256 devices in a mesh: dp: 8 (over z), seq: 32 (over x, y, core).
Axes of the slice: x: 4, y: 4, z: 8, core: 2. Of those that a mesh axis runs over, the one named last changes fastest.
Arguments:
- slide_tiles: bfloat16 [512, 256, 384], P(('dp', 'seq')), parts along dimension 0, may hold values from -6 to 6
- norm_gain: float32 [2, 384], replicated, may hold values from 0.1 to 1.9
- in_weight: bfloat16 [2, 384, 1536], replicated, may hold values from -0.3125 to 0.3125
- state_weight: bfloat16 [2, 384, 44], replicated, may hold values from -0.3125 to 0.3125
- conv_weight: float32 [2, 4, 800], replicated, may hold values from -2.5 to 2.5
- conv_bias: float32 [2, 800], replicated, may hold values from -0.5 to 0.5
- step_bias: float32 [2, 12], replicated, may hold values from -5 to -3
- decay_log: float32 [2, 12], replicated, may hold values from -8.5 to 1
- skip_gain: float32 [2, 12], replicated, may hold values from 0.5 to 1.5
- out_gain: float32 [2, 768], replicated, may hold values from 0.1 to 1.9
- out_weight: bfloat16 [2, 768, 384], replicated, may hold values from -0.21875 to 0.21875
Outputs:
- tile_out: bfloat16 [512, 256, 384], P(('dp', 'seq')), parts along dimension 0
The draws below stay inside these ranges and needn't reach their ends.
There are 8 independent parts, one for each index of `dp`. The reference program is written for one: setup_inputs(seed, part) draws one part's arguments, and reference() takes and returns one part's arrays. A program takes and returns all parts, laid end to end along the dimension named above; an argument that names none is the same for every part. Nothing has to cross between parts.
All inputs are finite; a program needn't handle non-finite values.
Results may differ from the reference program's by a relative error of at most 0.014.
Values may be sent and summed in bfloat16 or wider, within the bound.
No kernel may reach another device: no remote copies, remote signals or barrier semaphores. Data moves between devices by JAX's collectives and lax.ppermute only.
A program may use at most 64 MiB of HBM per device.

```python
import jax
import jax.numpy as jnp
from jax import lax

D = 384
HEADS = 12
HEADDIM = 64
STATE = 16
KERNEL = 4
GROUP = 256
COLS = 256
INNER = 768
ROWS = 64


def draw_decay_log(key, part):
    values = jax.random.uniform(key, (2, HEADS), jnp.float32, -8.5, 1.0)
    return values


def shard_levels(key, dims, cuts, least, top_value):
    loudness = 1.0
    for dim, parts in cuts:
        draws = jax.random.uniform(jax.random.fold_in(jax.random.fold_in(key, 6), dim), (parts,), jnp.float32, least / len(cuts), top_value / len(cuts))
        loudness = loudness * jnp.repeat(jnp.exp(draws), dims[dim] // parts).reshape((-1,) + (1,) * (len(dims) - 1 - dim))
    return loudness


def scatter_about(own_key, dims, deviation, most, shards=(), kind=jnp.bfloat16):
    entries = jax.random.normal(own_key, dims, jnp.float32) * deviation
    if len(shards) > 0:
        entries = shard_levels(own_key, dims, shards, -0.22, 0.18) * entries
    return jnp.clip(entries, min=-most, max=most).astype(kind)


def setup_inputs(seed: int = 0, part: int = 0) -> dict:
    streams_of = jax.random.split(jax.random.key(seed), 12)
    part_splits = jax.random.split(jax.random.fold_in(streams_of[11], part), 12)
    return {
        "slide_tiles": scatter_about(part_splits[0], (ROWS, COLS, D), 1.0, 6.0, ((0, 32),)),
        "norm_gain": jnp.clip(1.0 + 0.18 * jax.random.normal(streams_of[1], (2, D), jnp.float32), 0.1, 1.9),
        "in_weight": scatter_about(streams_of[2], (2, D, 2 * INNER), D ** -0.5, 0.3125),
        "state_weight": scatter_about(streams_of[3], (2, D, 2 * STATE + HEADS), D ** -0.5, 0.3125),
        "conv_weight": scatter_about(streams_of[4], (2, KERNEL, INNER + 2 * STATE), 0.5, 2.5, (), jnp.float32),
        "conv_bias": jnp.clip(jax.random.uniform(streams_of[5], (2, INNER + 2 * STATE), jnp.float32, -0.5, 0.5), -0.5, 0.5),
        "step_bias": jnp.clip(jax.random.uniform(streams_of[6], (2, HEADS), jnp.float32, -5.0, -3.0), -5.0, -3.0),
        "decay_log": draw_decay_log(jax.random.fold_in(streams_of[11], 71), part),
        "skip_gain": jnp.clip(jax.random.uniform(streams_of[8], (2, HEADS), jnp.float32, 0.5, 1.5), 0.5, 1.5),
        "out_gain": jnp.clip(1.0 + 0.18 * jax.random.normal(streams_of[9], (2, INNER), jnp.float32), 0.1, 1.9),
        "out_weight": scatter_about(streams_of[10], (2, INNER, D), INNER ** -0.5, 0.21875),
    }


epsilon = 1e-05

def rms_scaled(values, scale_gain):
    values = values.astype(jnp.float32)
    return values * lax.rsqrt(lax.optimization_barrier(jnp.mean(values * values, axis=-1, keepdims=True)) + epsilon) * scale_gain

def group_update(carry_state, group_in):
    group_x, group_b, group_c, group_step, group_rate = group_in
    cumulative = jnp.cumsum(group_rate, axis=0)
    positions = jnp.arange(group_x.shape[0])
    lower_mask = positions[:, None] >= positions[None, :]
    cum_heads = cumulative.T
    differences = cum_heads[:, :, None] - cum_heads[:, None, :]
    decay_mask = jnp.exp(jnp.where(lower_mask[None], differences, -jnp.inf))
    scores = jnp.dot(group_c, group_b.T, preferred_element_type=jnp.float32)
    weights = (scores[None] * decay_mask * group_step.T[:, None, :]).astype(jnp.bfloat16)
    intra_out = jnp.einsum('hts,shp->thp', weights.astype(jnp.float32), group_x.astype(jnp.float32))
    inter_out = jnp.exp(cumulative)[:, :, None] * jnp.einsum('tn,hpn->thp', group_c.astype(jnp.float32), carry_state, precision=lax.Precision.HIGHEST)
    tail_weight = jnp.exp(cumulative[-1][None, :] - cumulative) * group_step
    weighted_x = (group_x.astype(jnp.float32) * tail_weight[:, :, None]).astype(jnp.bfloat16)
    local_state = jnp.einsum('shp,sn->hpn', weighted_x.astype(jnp.float32), group_b.astype(jnp.float32))
    next_state = jnp.exp(cumulative[-1])[:, None, None] * carry_state + local_state
    return (next_state, intra_out + inter_out)

def mixer(sequence, layer, norm_gain, in_weight, state_weight, conv_weight, conv_bias, step_bias, decay_log, skip_gain, out_gain):
    length = sequence.shape[0]
    inner_width = in_weight.shape[2] // 2
    normed = rms_scaled(sequence, norm_gain[layer]).astype(jnp.bfloat16)
    gate_x = jnp.dot(normed, in_weight[layer], preferred_element_type=jnp.float32).astype(jnp.bfloat16)
    state_proj = jnp.dot(normed, state_weight[layer], preferred_element_type=jnp.float32).astype(jnp.bfloat16)
    conv_in = jnp.concatenate([gate_x[:, inner_width:], state_proj[:, :2 * STATE]], axis=1)
    margin = conv_weight.shape[1] - 1
    padded = jnp.concatenate([jnp.zeros((margin, conv_in.shape[1]), jnp.bfloat16), conv_in], axis=0)
    conv_sum = jnp.zeros((length, conv_in.shape[1]), jnp.float32) + conv_bias[layer][None, :]
    for offset in range(margin + 1):
        conv_sum = conv_sum + conv_weight[layer, offset][None, :] * padded[offset:offset + length].astype(jnp.float32)
    conv_out = jax.nn.silu(conv_sum).astype(jnp.bfloat16)
    x_conv = conv_out[:, :inner_width]
    b_conv = conv_out[:, inner_width:inner_width + STATE]
    c_conv = conv_out[:, inner_width + STATE:]
    step_size = jax.nn.softplus(state_proj[:, 2 * STATE:].astype(jnp.float32) + step_bias[layer][None, :])
    log_rates = -step_size * jnp.exp(decay_log[layer])[None, :]
    group_count = length // GROUP
    inputs = (x_conv.reshape(group_count, GROUP, HEADS, HEADDIM), b_conv.reshape(group_count, GROUP, STATE), c_conv.reshape(group_count, GROUP, STATE), step_size.reshape(group_count, GROUP, HEADS), log_rates.reshape(group_count, GROUP, HEADS))
    final_state, outputs = lax.scan(group_update, jnp.zeros((HEADS, HEADDIM, STATE), jnp.float32), inputs)
    y_total = outputs.reshape(length, HEADS, HEADDIM)
    y_total = y_total + skip_gain[layer][None, :, None] * x_conv.reshape(length, HEADS, HEADDIM).astype(jnp.float32)
    gated = y_total.reshape(length, inner_width) * jax.nn.silu(gate_x[:, :inner_width].astype(jnp.float32))
    return rms_scaled(gated, out_gain[layer]).astype(jnp.bfloat16)

def reference(slide_tiles, norm_gain, in_weight, state_weight, conv_weight, conv_bias, step_bias, decay_log, skip_gain, out_gain, out_weight):
    row_count, col_count, feature_count = slide_tiles.shape
    params = (norm_gain, in_weight, state_weight, conv_weight, conv_bias, step_bias, decay_log, skip_gain, out_gain)
    first_order = jnp.transpose(slide_tiles, (1, 0, 2)).reshape(row_count * col_count, feature_count)[::-1]
    mixed_out = mixer(first_order, 0, *params)
    after_first = (first_order.astype(jnp.float32) + jnp.dot(mixed_out, out_weight[0], preferred_element_type=jnp.float32)).astype(jnp.bfloat16)
    row_grid = jnp.transpose(after_first[::-1].reshape(col_count, row_count, feature_count), (1, 0, 2))
    second = row_grid.reshape(row_count * col_count, feature_count)
    mixed_out = mixer(second, 1, *params)
    result = (second.astype(jnp.float32) + jnp.dot(mixed_out, out_weight[1], preferred_element_type=jnp.float32)).astype(jnp.bfloat16)
    return result.reshape(row_count, col_count, feature_count)
```

```python
import functools

import jax
import jax.numpy as jnp
from jax import lax
from jax.experimental import pallas as pl
from jax.experimental.pallas import tpu as pltpu
from jax.sharding import PartitionSpec as P

D = 384
INNER = 768
HEADS = 12
HEADDIM = 64
STATE = 16
GROUP = 256
TOKENS = 512
PEERS = 32
CHUNK = 24
STATE_ROWS = 104
EPS = 1e-05
BF = jnp.bfloat16
F32 = jnp.float32
EXACT = lax.Precision.HIGHEST


def iota(shape, dim):
    return lax.broadcasted_iota(jnp.int32, shape, dim)


def dot(a, b, precision=None):
    return lax.dot_general(
        a, b, (((1,), (0,)), ((), ())), precision=precision, preferred_element_type=F32
    )


def dot_rows(a, b):
    return lax.dot_general(a, b, (((1,), (1,)), ((), ())), preferred_element_type=F32)


def one_hot(shape, column):
    return jnp.where(iota(shape, 1) == column, 1.0, 0.0).astype(BF)


def silu(v):
    half = 0.5 * v
    return half + half * jnp.tanh(half)


def rms(values, gain):
    return values * lax.rsqrt(jnp.mean(values * values, axis=-1, keepdims=True) + EPS) * gain


def in_two(values):
    high = values.astype(BF)
    return high, (values - high.astype(F32)).astype(BF)


def spread(values, width):
    lanes = HEADS * width
    shift = width.bit_length() - 1
    mask = lax.shift_right_logical(iota((16, lanes), 1), shift) == iota((16, lanes), 0)
    return dot(values, jnp.where(mask, 1.0, 0.0), EXACT)


def pack_body(tiles_ref, send_ref):
    rows = [tiles_ref[r].astype(F32).reshape(PEERS, 8, D) for r in range(2)]
    after = [jnp.concatenate([r[1:], jnp.zeros((1, 8, D), F32)], axis=0) for r in rows]
    place = iota((PEERS, 8, D), 1)
    second = jnp.concatenate([after[1][:, :1], after[1][:, :1]], axis=1)
    halo = jnp.where(
        place == 0,
        after[0],
        jnp.where(place == 1, jnp.broadcast_to(second[:, :1], (PEERS, 8, D)), 0.0),
    )
    send_ref[...] = jnp.concatenate([rows[0], rows[1], halo], axis=1).astype(BF)


def front_body(
    layer,
    recv_ref,
    gain_ref,
    wx_ref,
    ws_ref,
    cw_ref,
    cb_ref,
    col_ref,
    xs_ref,
    nm_ref,
    xc_ref,
    bt_ref,
    cc_ref,
    cum_ref,
    rt_ref,
    loc_ref,
    dec_ref,
    send_ref,
    conv_ref,
):
    main = recv_ref[:, 0:16, :].reshape(TOKENS, D)
    t = iota((TOKENS, 1), 0)
    if layer == 0:
        column = 511 - 8 * jnp.bitwise_and(t, 63) - lax.shift_right_logical(t, 6)
        halo_in = jnp.concatenate(
            [recv_ref[0, 16:24, :].astype(F32), recv_ref[1, 16:24, :].astype(F32)], axis=0
        )
        place = iota((16, 1), 0)
        picked = jnp.where(
            place == 13, 8, jnp.where(place == 14, 1, jnp.where(place == 15, 0, -1))
        )
    else:
        low = jnp.bitwise_and(t, 7)
        column = (
            2 * (jnp.bitwise_and(t, 255) - low) + 8 * lax.shift_right_logical(t, 8) + low
        )
        halo_in = jnp.concatenate(
            [recv_ref[PEERS - 1, 16:24, :].astype(F32), jnp.zeros((8, D), F32)], axis=0
        )
        place = iota((16, 1), 0)
        picked = jnp.where(place >= 13, place - 13, -1)
    xs = dot(one_hot((TOKENS, TOKENS), column), main)
    halo = dot(one_hot((16, 16), picked), halo_in.astype(BF))
    xs_ref[...] = xs.astype(BF)
    gain = gain_ref[layer : layer + 1, :]
    normed = rms(xs, gain).astype(BF)
    halo_normed = rms(halo, gain).astype(BF)
    nm_ref[...] = normed
    wx = wx_ref[0]
    conv_ref[8 : 8 + TOKENS, :] = dot(normed, wx).astype(BF).astype(F32)
    conv_ref[0:8, :] = dot(halo_normed, wx).astype(BF).astype(F32)[8:16]
    for block in range(INNER // 128):
        lanes = slice(128 * block, 128 * block + 128)
        total = cb_ref[layer : layer + 1, lanes] + cw_ref[layer, 0:1, lanes] * conv_ref[
            5 : 5 + TOKENS, lanes
        ]
        for tap in range(1, 4):
            total = total + cw_ref[layer, tap : tap + 1, lanes] * conv_ref[
                5 + tap : 5 + tap + TOKENS, lanes
            ]
        xc_ref[:, lanes] = silu(total).astype(BF)

    tall = jnp.concatenate([normed, jnp.zeros((112, D), BF), halo_normed], axis=0)
    proj = dot_rows(ws_ref[layer], tall).astype(BF).astype(F32)
    col = col_ref[layer]
    bc_in = proj[0:32, :]
    bc = col[0:32, 4:5] + col[0:32, 3:4] * bc_in
    for back in range(1, 4):
        bc = bc + col[0:32, 3 - back : 4 - back] * pltpu.roll(bc_in, back, 1)
    bc = silu(bc[:, 0:TOKENS])
    bt = bc[0:16]
    bt_ref[...] = bt.astype(BF)
    cc_ref[...] = bc.T[:, 16:32].astype(BF)

    raw = proj[32:48, 0:TOKENS] + col[32:48, 5:6]
    step = jnp.maximum(raw, 0.0) + jnp.log1p(jnp.exp(-jnp.abs(raw)))
    rate = -step * jnp.exp(col[32:48, 6:7])
    upper = jnp.where(iota((GROUP, GROUP), 0) <= iota((GROUP, GROUP), 1), 1.0, 0.0)
    cums = [dot(rate[:, g * GROUP : (g + 1) * GROUP], upper, EXACT) for g in range(2)]
    cum_rows = jnp.concatenate(cums, axis=1)
    rt = cum_rows - jnp.log(step)
    rt_ref[...] = rt
    cum = cum_rows.T
    cum_ref[...] = cum
    totals = jnp.concatenate([cum[255:256], cum[511:512], jnp.zeros((6, 16), F32)], axis=0)
    decays = spread(jnp.exp(totals), HEADDIM)
    dec_ref[...] = decays
    bt_held = bt.astype(BF).astype(F32)
    head = lax.shift_right_logical(iota((16, INNER), 1), 6)
    locals_ = []
    for g in range(2):
        span = slice(g * GROUP, (g + 1) * GROUP)
        tail = jnp.exp(cums[g][:, GROUP - 1 : GROUP] - rt[:, span])
        tilted = jnp.concatenate(
            [bt_held[:, span] * tail[h : h + 1, :] for h in range(HEADS)], axis=0
        ).astype(BF)
        every = dot(tilted, xc_ref[span, :])
        local = every[0:16]
        for h in range(1, HEADS):
            local = jnp.where(head == h, every[16 * h : 16 * h + 16], local)
        locals_.append(local)
    loc_ref[...] = locals_[0]
    final = (decays[1:2] * locals_[0] + locals_[1]).astype(BF)
    total = totals[0:1] + totals[1:2]
    high, low = in_two(total)
    pad = jnp.zeros((1, 112), F32)
    decay_rows = jnp.concatenate(
        [
            jnp.concatenate([high.astype(F32), pad], axis=1),
            jnp.concatenate([low.astype(F32), pad], axis=1),
            jnp.zeros((6, 128), F32),
        ],
        axis=0,
    )
    packed = jnp.concatenate(
        [final[:, 128 * b : 128 * b + 128].astype(F32) for b in range(6)] + [decay_rows], axis=0
    ).astype(BF)
    for peer in range(PEERS):
        send_ref[peer] = packed


def middle_body(
    layer, nm_ref, wz_ref, xc_ref, bt_ref, cc_ref, cum_ref, rt_ref, skip_ref, z_ref, y_ref, ct_ref
):
    z_ref[...] = dot(nm_ref[...], wz_ref[0]).astype(BF)
    held = cc_ref[...]
    mask = jnp.bitwise_and(iota((16, 192), 1), 15) == iota((16, 192), 0)
    repeated = dot(held, jnp.where(mask, 1.0, 0.0).astype(BF))
    ct_ref[...] = (repeated * spread(jnp.exp(cum_ref[...]), STATE)).astype(BF)
    skip = spread(jnp.broadcast_to(skip_ref[layer : layer + 1, :], (8, 16)), HEADDIM)
    half = GROUP // 2
    lower = iota((half, half), 0) >= iota((half, half), 1)
    left = iota((1, 128), 1) < HEADDIM
    for g in range(2):
        base = g * GROUP
        scores = dot(held[base : base + GROUP], bt_ref[:, base : base + GROUP])
        s00 = jnp.where(lower, scores[:half, :half], 0.0)
        s10 = scores[half:, :half]
        s11 = jnp.where(lower, scores[half:, half:], 0.0)
        for pair in range(HEADS // 2):
            lanes = slice(128 * pair, 128 * pair + 128)
            x = xc_ref[base : base + GROUP, lanes].astype(F32)
            top, low, inputs0, inputs1 = [], [], [], []
            for which in range(2):
                h = 2 * pair + which
                c0 = cum_ref[base : base + half, h : h + 1]
                c1 = cum_ref[base + half : base + GROUP, h : h + 1]
                r0 = rt_ref[h : h + 1, base : base + half]
                r1 = rt_ref[h : h + 1, base + half : base + GROUP]
                top.append((s00 * jnp.exp(jnp.minimum(c0 - r0, 80.0))).astype(BF))
                low.append((s10 * jnp.exp(c1 - r0)).astype(BF))
                low.append((s11 * jnp.exp(jnp.minimum(c1 - r1, 80.0))).astype(BF))
                own = jnp.where(left if which == 0 else ~left, x, 0.0).astype(BF)
                inputs0.append(own[:half])
                inputs1.append(own)
            y0 = dot(jnp.concatenate(top, axis=1), jnp.concatenate(inputs0, axis=0))
            y1 = dot(jnp.concatenate(low, axis=1), jnp.concatenate(inputs1, axis=0))
            weight = skip[0:1, lanes]
            y_ref[base : base + half, lanes] = y0 + weight * x[:half]
            y_ref[base + half : base + GROUP, lanes] = y1 + weight * x[half:]


def finish_body(
    layer,
    place_ref,
    recv_ref,
    loc_ref,
    dec_ref,
    z_ref,
    y_ref,
    ct_ref,
    xs_ref,
    gain_ref,
    wo_ref,
    out_ref,
):
    place = place_ref[0]
    decays = jnp.sum(recv_ref[:, 96:104, :].astype(F32), axis=1)
    source, between = iota((PEERS, PEERS), 0), iota((PEERS, PEERS), 1)
    if layer == 0:
        link = (between > place) & (between < source)
        valid = iota((PEERS, 128), 0) > place
    else:
        link = (between < place) & (between > source)
        valid = iota((PEERS, 128), 0) < place
    passed = dot(jnp.where(link, 1.0, 0.0), decays, EXACT)
    factor = jnp.where(valid, jnp.exp(passed), 0.0)
    mask = lax.shift_right_logical(iota((128, INNER), 1), 6) == iota((128, INNER), 0)
    factors = dot(factor, jnp.where(mask, 1.0, 0.0), EXACT)
    blocks = []
    for b in range(6):
        lanes = slice(128 * b, 128 * b + 128)
        total = jnp.zeros((16, 128), F32)
        for peer in range(PEERS):
            total = total + factors[peer : peer + 1, lanes] * recv_ref[
                peer, 16 * b : 16 * b + 16, :
            ].astype(F32)
        blocks.append(total)
    start = jnp.concatenate(blocks, axis=1)
    starts = [start, dec_ref[0:1, :] * start + loc_ref[...]]
    own = lax.shift_right_logical(iota((192, INNER), 1), 6) == lax.shift_right_logical(
        iota((192, INNER), 0), 4
    )
    mixed = []
    for g in range(2):
        span = slice(g * GROUP, (g + 1) * GROUP)
        wide = jnp.where(own, jnp.concatenate([starts[g]] * HEADS, axis=0), 0.0).astype(BF)
        y = y_ref[span, :] + dot(ct_ref[span, :], wide)
        gated = y * silu(z_ref[span, :].astype(F32))
        mixed.append(rms(gated, gain_ref[layer : layer + 1, :]).astype(BF))
    result = (
        xs_ref[...].astype(F32) + dot(jnp.concatenate(mixed, axis=0), wo_ref[0])
    ).astype(BF)
    if layer == 1:
        out_ref[...] = result
        return
    row = iota((PEERS * CHUNK, 1), 0)
    peer = lax.shift_right_logical(row * 2731, 16)
    slot = row - CHUNK * peer
    token = (7 - jnp.bitwise_and(slot, 7)) * 64 + 63 - 2 * peer - lax.shift_right_logical(slot, 3)
    edge = (18 - slot) * 64 + 64 - 2 * peer
    token = jnp.where(slot < 16, token, jnp.where((slot < 19) & (peer > 0), edge, -1))
    out_ref[...] = (
        dot(one_hot((PEERS * CHUNK, TOKENS), token), result)
        .reshape(PEERS, CHUNK, D)
        .astype(BF)
    )


def layer_half(which, axis_size):
    return pl.BlockSpec((1, D, INNER), lambda *_: (which[0], 0, which[1]))


def shaped(shape, dtype):
    return jax.ShapeDtypeStruct(shape, dtype)


def whole(a):
    return pl.BlockSpec(a.shape, lambda *_: (0,) * len(a.shape))


def call(body, args, specs, outs, flops, scratch=(), many=True):
    moved = sum(a.size * a.dtype.itemsize for a in args) + sum(
        o.size * o.dtype.itemsize for o in outs
    )
    return pl.pallas_call(
        body,
        grid=(1,),
        out_shape=tuple(outs) if many else outs[0],
        in_specs=[whole(a) if s is None else s for a, s in zip(args, specs)],
        out_specs=tuple(whole(o) for o in outs) if many else whole(outs[0]),
        scratch_shapes=list(scratch),
        compiler_params=pltpu.CompilerParams(vmem_limit_bytes=40 * 1024 * 1024),
        cost_estimate=pl.CostEstimate(flops=flops, bytes_accessed=moved, transcendentals=0),
    )(*args)


def exchange(chunks):
    return lax.all_to_all(chunks, "seq", 0, 0, tiled=True)


def run_layer(layer, received, place, params):
    gain, in_weight, ws, conv_weight, conv_bias, cols, skip, out_gain, out_weight = params
    fronts = call(
        functools.partial(front_body, layer),
        (received, gain, in_weight, ws, conv_weight, conv_bias, cols),
        (None, None, layer_half((layer, 1), 0), None, None, None, None),
        (
            shaped((TOKENS, D), BF),
            shaped((TOKENS, D), BF),
            shaped((TOKENS, INNER), BF),
            shaped((16, TOKENS), BF),
            shaped((TOKENS, 16), BF),
            shaped((TOKENS, 16), F32),
            shaped((16, TOKENS), F32),
            shaped((16, INNER), F32),
            shaped((8, INNER), F32),
            shaped((PEERS, STATE_ROWS, 128), BF),
        ),
        1_000_000_000,
        [pltpu.VMEM((TOKENS + 8, INNER), F32)],
    )
    xs, normed, xc, bt, cc, cum, rt, local, decays, send = fronts
    arrived = exchange(send)
    z, y, ct = call(
        functools.partial(middle_body, layer),
        (normed, in_weight, xc, bt, cc, cum, rt, skip),
        (None, layer_half((layer, 0), 0)) + (None,) * 6,
        (
            shaped((TOKENS, INNER), BF),
            shaped((TOKENS, INNER), F32),
            shaped((TOKENS, 192), BF),
        ),
        1_000_000_000,
    )
    out = shaped((TOKENS, D), BF) if layer else shaped((PEERS, CHUNK, D), BF)
    args = (place, arrived, local, decays, z, y, ct, xs, out_gain, out_weight)
    specs = [pl.BlockSpec(memory_space=pltpu.SMEM)] + [None] * 8
    specs.append(pl.BlockSpec((1, INNER, D), lambda *_: (layer, 0, 0)))
    return call(
        functools.partial(finish_body, layer), args, specs, (out,), 1_000_000_000, many=False
    )


def on_device(
    slide_tiles,
    norm_gain,
    in_weight,
    state_weight,
    conv_weight,
    conv_bias,
    step_bias,
    decay_log,
    skip_gain,
    out_gain,
    out_weight,
):
    place = lax.axis_index("seq").astype(jnp.int32).reshape(1)
    ws = jnp.pad(jnp.swapaxes(state_weight, 1, 2), ((0, 0), (0, 4), (0, 0)))
    conv_cols = jnp.concatenate(
        [
            jnp.swapaxes(conv_weight[:, :, INNER:], 1, 2),
            conv_bias[:, INNER:, None],
            jnp.zeros((2, 32, 3), F32),
        ],
        axis=2,
    )
    head_cols = jnp.stack([step_bias, decay_log], axis=2)
    head_cols = jnp.pad(head_cols, ((0, 0), (0, 4), (5, 1)))
    cols = jnp.concatenate([conv_cols, head_cols], axis=1)
    skip = jnp.pad(skip_gain, ((0, 0), (0, 4)))
    params = (
        norm_gain,
        in_weight,
        ws,
        conv_weight,
        conv_bias,
        cols,
        skip,
        out_gain,
        out_weight,
    )
    send = call(
        pack_body,
        (slide_tiles,),
        (None,),
        (shaped((PEERS, CHUNK, D), BF),),
        1_000_000,
        many=False,
    )
    middle = run_layer(0, exchange(send), place, params)
    result = run_layer(1, exchange(middle), place, params)
    return result.reshape(slide_tiles.shape)


def solution(mesh):
    placed = (P(("dp", "seq"), None, None), P(), P(), P(), P(), P(), P(), P(), P(), P(), P())
    return jax.shard_map(
        on_device,
        mesh=mesh,
        in_specs=placed,
        out_specs=P(("dp", "seq"), None, None),
        check_vma=False,
    )
```

```python
import functools
import math

import jax
import jax.numpy as jnp
from jax import lax
from jax.experimental import pallas as pl
from jax.experimental.pallas import tpu as pltpu
from jax.sharding import PartitionSpec as P

D = 384
INNER = 768
HEADS = 12
HEADDIM = 64
STATE = 16
GROUP = 256
TOKENS = 512
PEERS = 32
CHUNK = 24
STATE_ROWS = 104
EPS = 1e-05
BF = jnp.bfloat16
F32 = jnp.float32
EXACT = lax.Precision.HIGHEST


def iota(shape, dim):
    return lax.broadcasted_iota(jnp.int32, shape, dim)


def dot(a, b, precision=None):
    return lax.dot_general(
        a, b, (((1,), (0,)), ((), ())), precision=precision, preferred_element_type=F32
    )


def dot_rows(a, b):
    return lax.dot_general(a, b, (((1,), (1,)), ((), ())), preferred_element_type=F32)


def one_hot(shape, column):
    return jnp.where(iota(shape, 1) == column, 1.0, 0.0).astype(BF)


def silu(v):
    half = 0.5 * v
    return half + half * jnp.tanh(half)


def rms(values, gain):
    return values * lax.rsqrt(jnp.mean(values * values, axis=-1, keepdims=True) + EPS) * gain


def in_two(values):
    high = values.astype(BF)
    return high, (values - high.astype(F32)).astype(BF)


def spread(values, width):
    lanes = HEADS * width
    shift = width.bit_length() - 1
    mask = lax.shift_right_logical(iota((16, lanes), 1), shift) == iota((16, lanes), 0)
    return dot(values, jnp.where(mask, 1.0, 0.0), EXACT)


def pack_body(tiles_ref, send_ref):
    halo = jnp.zeros((PEERS, 8, 128), F32)
    slot = iota((PEERS, 8, 128), 1)
    for b in range(3):
        lanes = slice(128 * b, 128 * b + 128)
        rows = [tiles_ref[r, :, lanes].astype(F32).reshape(PEERS, 8, 128) for r in range(2)]
        send_ref[:, 16 * b : 16 * b + 16, :] = jnp.concatenate(rows, axis=1).astype(BF)
        for r in range(2):
            after = jnp.concatenate([rows[r][1:, 0:1], jnp.zeros((1, 1, 128), F32)], axis=0)
            halo = jnp.where(slot == 2 * b + r, after, halo)
    send_ref[:, 48:56, :] = halo.astype(BF)


def front_body(
    layer,
    recv_ref,
    gain_ref,
    wx_ref,
    ws_ref,
    cw_ref,
    cb_ref,
    col_ref,
    xs_ref,
    nm_ref,
    xc_ref,
    bt_ref,
    cc_ref,
    cum_ref,
    rt_ref,
    loc_ref,
    dec_ref,
    send_ref,
    conv_ref,
):
    t = iota((TOKENS, 1), 0)
    place = iota((16, 1), 0)
    if layer == 0:
        main = jnp.concatenate(
            [recv_ref[:, 16 * b : 16 * b + 16, :].reshape(TOKENS, 128) for b in range(3)], axis=1
        )
        column = 511 - 8 * jnp.bitwise_and(t, 63) - lax.shift_right_logical(t, 6)
        halo_in = jnp.concatenate(
            [recv_ref[0, 48:56, :].astype(F32), recv_ref[1, 48:56, :].astype(F32)], axis=0
        ).astype(BF)
        picked = jnp.where(
            place == 13, 8, jnp.where(place == 14, 1, jnp.where(place == 15, 0, -16))
        )
        halo = jnp.concatenate(
            [dot(one_hot((16, 16), picked + 2 * b), halo_in) for b in range(3)], axis=1
        )
    else:
        main = recv_ref[:, 0:16, :].reshape(TOKENS, D)
        low = jnp.bitwise_and(t, 7)
        column = (
            2 * (jnp.bitwise_and(t, 255) - low) + 8 * lax.shift_right_logical(t, 8) + low
        )
        halo_in = jnp.concatenate(
            [recv_ref[PEERS - 1, 16:24, :].astype(F32), jnp.zeros((8, D), F32)], axis=0
        ).astype(BF)
        halo = dot(one_hot((16, 16), jnp.where(place >= 13, place - 13, -1)), halo_in)
    xs = dot(one_hot((TOKENS, TOKENS), column), main)
    xs_ref[...] = xs.astype(BF)
    gain = gain_ref[layer : layer + 1, :]
    normed = rms(xs, gain).astype(BF)
    halo_normed = rms(halo, gain).astype(BF)
    nm_ref[...] = normed
    wx = wx_ref[0]
    conv_ref[8 : 8 + TOKENS, :] = dot(normed, wx).astype(BF).astype(F32)
    conv_ref[0:8, :] = dot(halo_normed, wx).astype(BF).astype(F32)[8:16]
    for block in range(INNER // 128):
        lanes = slice(128 * block, 128 * block + 128)
        total = cb_ref[layer : layer + 1, lanes] + cw_ref[layer, 0:1, lanes] * conv_ref[
            5 : 5 + TOKENS, lanes
        ]
        for tap in range(1, 4):
            total = total + cw_ref[layer, tap : tap + 1, lanes] * conv_ref[
                5 + tap : 5 + tap + TOKENS, lanes
            ]
        xc_ref[:, lanes] = silu(total).astype(BF)

    tall = jnp.concatenate([normed, jnp.zeros((112, D), BF), halo_normed], axis=0)
    proj = dot_rows(ws_ref[layer], tall).astype(BF).astype(F32)
    col = col_ref[layer]
    bc_in = proj[0:32, :]
    bc = col[0:32, 4:5] + col[0:32, 3:4] * bc_in
    for back in range(1, 4):
        bc = bc + col[0:32, 3 - back : 4 - back] * pltpu.roll(bc_in, back, 1)
    bc = silu(bc[:, 0:TOKENS])
    bt = bc[0:16]
    bt_ref[...] = bt.astype(BF)
    cc_ref[...] = bc.T[:, 16:32].astype(BF)

    raw = proj[32:48, 0:TOKENS] + col[32:48, 5:6]
    step = jnp.maximum(raw, 0.0) + jnp.log1p(jnp.exp(-jnp.abs(raw)))
    rate = -step * jnp.exp(col[32:48, 6:7])
    upper = jnp.where(iota((GROUP, GROUP), 0) <= iota((GROUP, GROUP), 1), 1.0, 0.0)
    cums = [dot(rate[:, g * GROUP : (g + 1) * GROUP], upper, EXACT) for g in range(2)]
    cum_rows = jnp.concatenate(cums, axis=1)
    rt = cum_rows - jnp.log(step)
    rt_ref[...] = rt
    cum = cum_rows.T
    cum_ref[...] = cum
    totals = jnp.concatenate([cum[255:256], cum[511:512], jnp.zeros((6, 16), F32)], axis=0)
    decays = spread(jnp.exp(totals), HEADDIM)
    dec_ref[...] = decays
    bt_held = bt.astype(BF).astype(F32)
    head = lax.shift_right_logical(iota((16, INNER), 1), 6)
    locals_ = []
    for g in range(2):
        span = slice(g * GROUP, (g + 1) * GROUP)
        tail = jnp.exp(cums[g][:, GROUP - 1 : GROUP] - rt[:, span])
        tilted = jnp.concatenate(
            [bt_held[:, span] * tail[h : h + 1, :] for h in range(HEADS)], axis=0
        ).astype(BF)
        every = dot(tilted, xc_ref[span, :])
        local = every[0:16]
        for h in range(1, HEADS):
            local = jnp.where(head == h, every[16 * h : 16 * h + 16], local)
        locals_.append(local)
    loc_ref[...] = locals_[0]
    final = (decays[1:2] * locals_[0] + locals_[1]).astype(BF)
    total = totals[0:1] + totals[1:2]
    high, low = in_two(total)
    pad = jnp.zeros((1, 112), F32)
    decay_rows = jnp.concatenate(
        [
            jnp.concatenate([high.astype(F32), pad], axis=1),
            jnp.concatenate([low.astype(F32), pad], axis=1),
            jnp.zeros((6, 128), F32),
        ],
        axis=0,
    )
    packed = jnp.concatenate(
        [final[:, 128 * b : 128 * b + 128].astype(F32) for b in range(6)] + [decay_rows], axis=0
    ).astype(BF)
    for peer in range(PEERS):
        send_ref[peer] = packed


def middle_body(
    layer, nm_ref, wz_ref, xc_ref, bt_ref, cc_ref, cum_ref, rt_ref, skip_ref, z_ref, y_ref, ct_ref
):
    z_ref[...] = dot(nm_ref[...], wz_ref[0]).astype(BF)
    held = cc_ref[...]
    mask = jnp.bitwise_and(iota((16, 192), 1), 15) == iota((16, 192), 0)
    repeated = dot(held, jnp.where(mask, 1.0, 0.0).astype(BF))
    ct_ref[...] = (repeated * spread(jnp.exp(cum_ref[...]), STATE)).astype(BF)
    skip = spread(jnp.broadcast_to(skip_ref[layer : layer + 1, :], (8, 16)), HEADDIM)
    half = GROUP // 2
    lower = iota((half, half), 0) >= iota((half, half), 1)
    left = iota((1, 128), 1) < HEADDIM
    for g in range(2):
        base = g * GROUP
        scores = dot(held[base : base + GROUP], bt_ref[:, base : base + GROUP])
        s00 = jnp.where(lower, scores[:half, :half], 0.0)
        s10 = scores[half:, :half]
        s11 = jnp.where(lower, scores[half:, half:], 0.0)
        for pair in range(HEADS // 2):
            lanes = slice(128 * pair, 128 * pair + 128)
            x = xc_ref[base : base + GROUP, lanes].astype(F32)
            top, low, inputs0, inputs1 = [], [], [], []
            for which in range(2):
                h = 2 * pair + which
                c0 = cum_ref[base : base + half, h : h + 1]
                c1 = cum_ref[base + half : base + GROUP, h : h + 1]
                r0 = rt_ref[h : h + 1, base : base + half]
                r1 = rt_ref[h : h + 1, base + half : base + GROUP]
                top.append((s00 * jnp.exp(jnp.minimum(c0 - r0, 80.0))).astype(BF))
                low.append((s10 * jnp.exp(c1 - r0)).astype(BF))
                low.append((s11 * jnp.exp(jnp.minimum(c1 - r1, 80.0))).astype(BF))
                own = jnp.where(left if which == 0 else ~left, x, 0.0).astype(BF)
                inputs0.append(own[:half])
                inputs1.append(own)
            y0 = dot(jnp.concatenate(top, axis=1), jnp.concatenate(inputs0, axis=0))
            y1 = dot(jnp.concatenate(low, axis=1), jnp.concatenate(inputs1, axis=0))
            weight = skip[0:1, lanes]
            y_ref[base : base + half, lanes] = y0 + weight * x[:half]
            y_ref[base + half : base + GROUP, lanes] = y1 + weight * x[half:]


def finish_body(
    layer,
    place_ref,
    recv_ref,
    loc_ref,
    dec_ref,
    z_ref,
    y_ref,
    ct_ref,
    xs_ref,
    gain_ref,
    wo_ref,
    out_ref,
):
    place = place_ref[0]
    decays = jnp.sum(recv_ref[:, 96:104, :].astype(F32), axis=1)
    source, between = iota((PEERS, PEERS), 0), iota((PEERS, PEERS), 1)
    if layer == 0:
        link = (between > place) & (between < source)
        valid = iota((PEERS, 128), 0) > place
    else:
        link = (between < place) & (between > source)
        valid = iota((PEERS, 128), 0) < place
    passed = dot(jnp.where(link, 1.0, 0.0), decays, EXACT)
    factor = jnp.where(valid, jnp.exp(passed), 0.0)
    mask = lax.shift_right_logical(iota((128, INNER), 1), 6) == iota((128, INNER), 0)
    factors = dot(factor, jnp.where(mask, 1.0, 0.0), EXACT)
    blocks = []
    for b in range(6):
        lanes = slice(128 * b, 128 * b + 128)
        total = jnp.zeros((16, 128), F32)
        for peer in range(PEERS):
            total = total + factors[peer : peer + 1, lanes] * recv_ref[
                peer, 16 * b : 16 * b + 16, :
            ].astype(F32)
        blocks.append(total)
    start = jnp.concatenate(blocks, axis=1)
    starts = [start, dec_ref[0:1, :] * start + loc_ref[...]]
    own = lax.shift_right_logical(iota((192, INNER), 1), 6) == lax.shift_right_logical(
        iota((192, INNER), 0), 4
    )
    mixed = []
    for g in range(2):
        span = slice(g * GROUP, (g + 1) * GROUP)
        wide = jnp.where(own, jnp.concatenate([starts[g]] * HEADS, axis=0), 0.0).astype(BF)
        y = y_ref[span, :] + dot(ct_ref[span, :], wide)
        gated = y * silu(z_ref[span, :].astype(F32))
        mixed.append(rms(gated, gain_ref[layer : layer + 1, :]).astype(BF))
    result = (
        xs_ref[...].astype(F32) + dot(jnp.concatenate(mixed, axis=0), wo_ref[0])
    ).astype(BF)
    if layer == 1:
        out_ref[...] = result
        return
    row = iota((PEERS * CHUNK, 1), 0)
    peer = lax.shift_right_logical(row * 2731, 16)
    slot = row - CHUNK * peer
    token = (7 - jnp.bitwise_and(slot, 7)) * 64 + 63 - 2 * peer - lax.shift_right_logical(slot, 3)
    edge = (18 - slot) * 64 + 64 - 2 * peer
    token = jnp.where(slot < 16, token, jnp.where((slot < 19) & (peer > 0), edge, -1))
    out_ref[...] = (
        dot(one_hot((PEERS * CHUNK, TOKENS), token), result)
        .reshape(PEERS, CHUNK, D)
        .astype(BF)
    )


def layer_half(which, axis_size):
    return pl.BlockSpec((1, D, INNER), lambda *_: (which[0], 0, which[1]))


def shaped(shape, dtype):
    return jax.ShapeDtypeStruct(shape, dtype)


def kept(shape, dtype):
    return pltpu.HBM(shape, dtype)


def pinned(*arrays):
    return tuple(pltpu.with_memory_space_constraint(a, pltpu.HBM) for a in arrays)


def whole(a):
    return pl.BlockSpec(a.shape, lambda *_: (0,) * len(a.shape))


def call(body, args, specs, outs, flops, scratch=(), many=True):
    moved = sum(a.size * a.dtype.itemsize for a in args) + sum(
        math.prod(o.shape) * jnp.dtype(o.dtype).itemsize for o in outs
    )
    return pl.pallas_call(
        body,
        grid=(1,),
        out_shape=tuple(outs) if many else outs[0],
        in_specs=[whole(a) if s is None else s for a, s in zip(args, specs)],
        out_specs=tuple(whole(o) for o in outs) if many else whole(outs[0]),
        scratch_shapes=list(scratch),
        compiler_params=pltpu.CompilerParams(vmem_limit_bytes=40 * 1024 * 1024),
        cost_estimate=pl.CostEstimate(flops=flops, bytes_accessed=moved, transcendentals=0),
    )(*args)


def exchange(chunks):
    return lax.all_to_all(chunks, "seq", 0, 0, tiled=True)


def run_layer(layer, received, place, params):
    gain, in_weight, ws, conv_weight, conv_bias, cols, skip, out_gain, out_weight = params
    fronts = call(
        functools.partial(front_body, layer),
        (received, gain, in_weight, ws, conv_weight, conv_bias, cols),
        (None, None, layer_half((layer, 1), 0), None, None, None, None),
        (
            kept((TOKENS, D), BF),
            kept((TOKENS, D), BF),
            kept((TOKENS, INNER), BF),
            kept((16, TOKENS), BF),
            kept((TOKENS, 16), BF),
            kept((TOKENS, 16), F32),
            kept((16, TOKENS), F32),
            kept((16, INNER), F32),
            kept((8, INNER), F32),
            kept((PEERS, STATE_ROWS, 128), BF),
        ),
        1_000_000_000,
        [pltpu.VMEM((TOKENS + 8, INNER), F32)],
    )
    xs, normed, xc, bt, cc, cum, rt, local, decays, send = pinned(*fronts)
    arrived = exchange(send)
    z, y, ct = pinned(*call(
        functools.partial(middle_body, layer),
        (normed, in_weight, xc, bt, cc, cum, rt, skip),
        (None, layer_half((layer, 0), 0)) + (None,) * 6,
        (
            kept((TOKENS, INNER), BF),
            kept((TOKENS, INNER), F32),
            kept((TOKENS, 192), BF),
        ),
        1_000_000_000,
    ))
    out = shaped((TOKENS, D), BF) if layer else shaped((PEERS, CHUNK, D), BF)
    args = (place, arrived, local, decays, z, y, ct, xs, out_gain, out_weight)
    specs = [pl.BlockSpec(memory_space=pltpu.SMEM)] + [None] * 8
    specs.append(pl.BlockSpec((1, INNER, D), lambda *_: (layer, 0, 0)))
    return call(
        functools.partial(finish_body, layer), args, specs, (out,), 1_000_000_000, many=False
    )


def on_device(
    slide_tiles,
    norm_gain,
    in_weight,
    state_weight,
    conv_weight,
    conv_bias,
    step_bias,
    decay_log,
    skip_gain,
    out_gain,
    out_weight,
):
    place = lax.axis_index("seq").astype(jnp.int32).reshape(1)
    ws = jnp.pad(jnp.swapaxes(state_weight, 1, 2), ((0, 0), (0, 4), (0, 0)))
    conv_cols = jnp.concatenate(
        [
            jnp.swapaxes(conv_weight[:, :, INNER:], 1, 2),
            conv_bias[:, INNER:, None],
            jnp.zeros((2, 32, 3), F32),
        ],
        axis=2,
    )
    head_cols = jnp.stack([step_bias, decay_log], axis=2)
    head_cols = jnp.pad(head_cols, ((0, 0), (0, 4), (5, 1)))
    cols = jnp.concatenate([conv_cols, head_cols], axis=1)
    skip = jnp.pad(skip_gain, ((0, 0), (0, 4)))
    params = (
        norm_gain,
        in_weight,
        ws,
        conv_weight,
        conv_bias,
        cols,
        skip,
        out_gain,
        out_weight,
    )
    send = call(
        pack_body,
        (slide_tiles,),
        (None,),
        (kept((PEERS, 56, 128), BF),),
        1_000_000,
        many=False,
    )
    middle = run_layer(0, exchange(send), place, params)
    result = run_layer(1, exchange(middle), place, params)
    return result.reshape(slide_tiles.shape)


def solution(mesh):
    placed = (P(("dp", "seq"), None, None), P(), P(), P(), P(), P(), P(), P(), P(), P(), P())
    return jax.shard_map(
        on_device,
        mesh=mesh,
        in_specs=placed,
        out_specs=P(("dp", "seq"), None, None),
        check_vma=False,
    )
```

```python
import functools
import math

import jax
import jax.numpy as jnp
from jax import lax
from jax.experimental import pallas as pl
from jax.experimental.pallas import tpu as pltpu
from jax.sharding import PartitionSpec as P

D = 384
INNER = 768
HEADS = 12
HEADDIM = 64
STATE = 16
GROUP = 256
TOKENS = 512
PEERS = 32
CHUNK = 24
STATE_ROWS = 104
EPS = 1e-05
BF = jnp.bfloat16
F32 = jnp.float32
EXACT = lax.Precision.HIGHEST


def iota(shape, dim):
    return lax.broadcasted_iota(jnp.int32, shape, dim)


def dot(a, b, precision=None):
    return lax.dot_general(
        a, b, (((1,), (0,)), ((), ())), precision=precision, preferred_element_type=F32
    )


def dot_rows(a, b):
    return lax.dot_general(a, b, (((1,), (1,)), ((), ())), preferred_element_type=F32)


def one_hot(shape, column):
    return jnp.where(iota(shape, 1) == column, 1.0, 0.0).astype(BF)


def silu(v):
    half = 0.5 * v
    return half + half * jnp.tanh(half)


def rms(values, gain):
    return values * lax.rsqrt(jnp.mean(values * values, axis=-1, keepdims=True) + EPS) * gain


def in_two(values):
    high = values.astype(BF)
    return high, (values - high.astype(F32)).astype(BF)


def spread(values, width):
    lanes = HEADS * width
    shift = width.bit_length() - 1
    mask = lax.shift_right_logical(iota((16, lanes), 1), shift) == iota((16, lanes), 0)
    return dot(values, jnp.where(mask, 1.0, 0.0), EXACT)


def pack_body(tiles_hbm, send_hbm, tiles_ref, send_ref, sems):
    load = pltpu.make_async_copy(tiles_hbm, tiles_ref, sems.at[0])
    load.start()
    load.wait()
    stores = []
    part = PEERS // 4
    slot = iota((part, 8, 128), 1)
    for q in range(4):
        halo = jnp.zeros((part, 8, 128), F32)
        for b in range(3):
            lanes = slice(128 * b, 128 * b + 128)
            first = 8 * part * q
            rows = [
                tiles_ref[r, first : first + 8 * part, lanes].astype(F32).reshape(part, 8, 128)
                for r in range(2)
            ]
            send_ref[part * q : part * q + part, 16 * b : 16 * b + 16, :] = jnp.concatenate(
                rows, axis=1
            ).astype(BF)
            for r in range(2):
                if q < 3:
                    beyond = tiles_ref[r, first + 8 * part : first + 8 * part + 16, lanes]
                    beyond = beyond.astype(F32)[0:1].reshape(1, 1, 128)
                else:
                    beyond = jnp.zeros((1, 1, 128), F32)
                after = jnp.concatenate([rows[r][1:, 0:1], beyond], axis=0)
                halo = jnp.where(slot == 2 * b + r, after, halo)
        send_ref[part * q : part * q + part, 48:56, :] = halo.astype(BF)
        own = pl.ds(part * q, part)
        store = pltpu.make_async_copy(send_ref.at[own], send_hbm.at[own], sems.at[1 + q])
        store.start()
        stores.append(store)
    for store in stores:
        store.wait()


def front_body(
    layer,
    recv_ref,
    gain_ref,
    wx_hbm,
    ws_ref,
    cw_ref,
    cb_ref,
    col_ref,
    xs_hbm,
    xc_hbm,
    rows_hbm,
    loc_hbm,
    send_hbm,
    wx_ref,
    conv_ref,
    xs_ref,
    xc_ref,
    rows_ref,
    loc_ref,
    chunk_ref,
    sems,
    send_sems,
):
    load = pltpu.make_async_copy(wx_hbm.at[layer, :, pl.ds(INNER, INNER)], wx_ref, sems.at[0])
    load.start()
    t = iota((TOKENS, 1), 0)
    place = iota((16, 1), 0)
    if layer == 0:
        main = jnp.concatenate(
            [recv_ref[:, 16 * b : 16 * b + 16, :].reshape(TOKENS, 128) for b in range(3)], axis=1
        )
        column = 511 - 8 * jnp.bitwise_and(t, 63) - lax.shift_right_logical(t, 6)
        halo_in = jnp.concatenate(
            [recv_ref[0, 48:56, :].astype(F32), recv_ref[1, 48:56, :].astype(F32)], axis=0
        ).astype(BF)
        picked = jnp.where(
            place == 13, 8, jnp.where(place == 14, 1, jnp.where(place == 15, 0, -16))
        )
        halo = jnp.concatenate(
            [dot(one_hot((16, 16), picked + 2 * b), halo_in) for b in range(3)], axis=1
        )
    else:
        main = recv_ref[:, 0:16, :].reshape(TOKENS, D)
        low = jnp.bitwise_and(t, 7)
        column = (
            2 * (jnp.bitwise_and(t, 255) - low) + 8 * lax.shift_right_logical(t, 8) + low
        )
        halo_in = jnp.concatenate(
            [recv_ref[PEERS - 1, 16:24, :].astype(F32), jnp.zeros((8, D), F32)], axis=0
        ).astype(BF)
        halo = dot(one_hot((16, 16), jnp.where(place >= 13, place - 13, -1)), halo_in)
    xs = dot(one_hot((TOKENS, TOKENS), column), main)
    xs_ref[...] = xs.astype(BF)
    stores = [pltpu.make_async_copy(xs_ref, xs_hbm, sems.at[1])]
    stores[0].start()
    gain = gain_ref[layer : layer + 1, :]
    normed = rms(xs, gain).astype(BF)
    halo_normed = rms(halo, gain).astype(BF)
    load.wait()
    wx = wx_ref[...]
    conv_ref[8 : 8 + TOKENS, :] = dot(normed, wx).astype(BF).astype(F32)
    conv_ref[0:8, :] = dot(halo_normed, wx).astype(BF).astype(F32)[8:16]
    for block in range(INNER // 128):
        lanes = slice(128 * block, 128 * block + 128)
        total = cb_ref[layer : layer + 1, lanes] + cw_ref[layer, 0:1, lanes] * conv_ref[
            5 : 5 + TOKENS, lanes
        ]
        for tap in range(1, 4):
            total = total + cw_ref[layer, tap : tap + 1, lanes] * conv_ref[
                5 + tap : 5 + tap + TOKENS, lanes
            ]
        xc_ref[:, lanes] = silu(total).astype(BF)
    stores.append(pltpu.make_async_copy(xc_ref, xc_hbm, sems.at[2]))
    stores[1].start()

    tall = jnp.concatenate([normed, jnp.zeros((112, D), BF), halo_normed], axis=0)
    proj = dot_rows(ws_ref[layer], tall).astype(BF).astype(F32)
    col = col_ref[layer]
    bc_in = proj[0:32, :]
    bc = col[0:32, 4:5] + col[0:32, 3:4] * bc_in
    for back in range(1, 4):
        bc = bc + col[0:32, 3 - back : 4 - back] * pltpu.roll(bc_in, back, 1)
    bc = silu(bc[:, 0:TOKENS])
    rows_ref[0:32, :] = bc.astype(BF).astype(F32)

    raw = proj[32:48, 0:TOKENS] + col[32:48, 5:6]
    step = jnp.maximum(raw, 0.0) + jnp.log1p(jnp.exp(-jnp.abs(raw)))
    rate = -step * jnp.exp(col[32:48, 6:7])
    upper = jnp.where(iota((GROUP, GROUP), 0) <= iota((GROUP, GROUP), 1), 1.0, 0.0)
    cums = [dot(rate[:, g * GROUP : (g + 1) * GROUP], upper, EXACT) for g in range(2)]
    cum_rows = jnp.concatenate(cums, axis=1)
    rt = cum_rows - jnp.log(step)
    rows_ref[32:48, :] = rt
    rows_ref[48:64, :] = cum_rows
    stores.append(pltpu.make_async_copy(rows_ref, rows_hbm, sems.at[3]))
    stores[2].start()
    ends = [jnp.broadcast_to(c[:, GROUP - 1 : GROUP], (16, 128)) for c in cums]
    ends = [e.T[0:1] for e in ends]
    totals = jnp.concatenate([ends[0], ends[1], jnp.zeros((6, 16), F32)], axis=0)
    decays = spread(jnp.exp(totals), HEADDIM)
    loc_ref[16:24, :] = decays
    bt_held = rows_ref[0:16, :]
    head = lax.shift_right_logical(iota((16, INNER), 1), 6)
    locals_ = []
    for g in range(2):
        span = slice(g * GROUP, (g + 1) * GROUP)
        tail = jnp.exp(cums[g][:, GROUP - 1 : GROUP] - rt[:, span])
        tilted = jnp.concatenate(
            [bt_held[:, span] * tail[h : h + 1, :] for h in range(HEADS)], axis=0
        ).astype(BF)
        every = dot(tilted, xc_ref[span, :])
        local = every[0:16]
        for h in range(1, HEADS):
            local = jnp.where(head == h, every[16 * h : 16 * h + 16], local)
        locals_.append(local)
    loc_ref[0:16, :] = locals_[0]
    stores.append(pltpu.make_async_copy(loc_ref, loc_hbm, sems.at[4]))
    stores[3].start()
    final = (decays[1:2] * locals_[0] + locals_[1]).astype(BF)
    total = totals[0:1] + totals[1:2]
    high, low = in_two(total)
    pad = jnp.zeros((1, 112), F32)
    decay_rows = jnp.concatenate(
        [
            jnp.concatenate([high.astype(F32), pad], axis=1),
            jnp.concatenate([low.astype(F32), pad], axis=1),
            jnp.zeros((6, 128), F32),
        ],
        axis=0,
    )
    chunk_ref[...] = jnp.concatenate(
        [final[:, 128 * b : 128 * b + 128].astype(F32) for b in range(6)] + [decay_rows], axis=0
    ).astype(BF)
    for peer in range(PEERS):
        stores.append(pltpu.make_async_copy(chunk_ref, send_hbm.at[peer], send_sems.at[peer]))
        stores[-1].start()
    for store in stores:
        store.wait()


def middle_body(
    layer, xs_ref, gain_ref, wz_ref, xc_ref, rows_ref, skip_ref, z_ref, y_ref, ct_ref, cum_ref
):
    normed = rms(xs_ref[...].astype(F32), gain_ref[layer : layer + 1, :]).astype(BF)
    z_ref[...] = dot(normed, wz_ref[0]).astype(BF)
    bt_ref = rows_ref[0:16, :].astype(BF)
    held = rows_ref[0:32, :].T[:, 16:32].astype(BF)
    cum_ref[...] = rows_ref[48:64, :].T
    mask = jnp.bitwise_and(iota((16, 192), 1), 15) == iota((16, 192), 0)
    repeated = dot(held, jnp.where(mask, 1.0, 0.0).astype(BF))
    ct_ref[...] = (repeated * spread(jnp.exp(cum_ref[...]), STATE)).astype(BF)
    skip = spread(jnp.broadcast_to(skip_ref[layer : layer + 1, :], (8, 16)), HEADDIM)
    half = GROUP // 2
    lower = iota((half, half), 0) >= iota((half, half), 1)
    left = iota((1, 128), 1) < HEADDIM
    for g in range(2):
        base = g * GROUP
        scores = dot(held[base : base + GROUP], bt_ref[:, base : base + GROUP])
        s00 = jnp.where(lower, scores[:half, :half], 0.0)
        s10 = scores[half:, :half]
        s11 = jnp.where(lower, scores[half:, half:], 0.0)
        for pair in range(HEADS // 2):
            lanes = slice(128 * pair, 128 * pair + 128)
            x = xc_ref[base : base + GROUP, lanes].astype(F32)
            top, low, inputs0, inputs1 = [], [], [], []
            for which in range(2):
                h = 2 * pair + which
                c0 = cum_ref[base : base + half, h : h + 1]
                c1 = cum_ref[base + half : base + GROUP, h : h + 1]
                r0 = rows_ref[32 + h : 33 + h, base : base + half]
                r1 = rows_ref[32 + h : 33 + h, base + half : base + GROUP]
                top.append((s00 * jnp.exp(jnp.minimum(c0 - r0, 80.0))).astype(BF))
                low.append((s10 * jnp.exp(c1 - r0)).astype(BF))
                low.append((s11 * jnp.exp(jnp.minimum(c1 - r1, 80.0))).astype(BF))
                own = jnp.where(left if which == 0 else ~left, x, 0.0).astype(BF)
                inputs0.append(own[:half])
                inputs1.append(own)
            y0 = dot(jnp.concatenate(top, axis=1), jnp.concatenate(inputs0, axis=0))
            y1 = dot(jnp.concatenate(low, axis=1), jnp.concatenate(inputs1, axis=0))
            weight = skip[0:1, lanes]
            y_ref[base : base + half, lanes] = y0 + weight * x[:half]
            y_ref[base + half : base + GROUP, lanes] = y1 + weight * x[half:]


def finish_body(
    layer,
    place_ref,
    recv_ref,
    loc_hbm,
    ct_hbm,
    y_hbm,
    z_hbm,
    xs_hbm,
    gain_ref,
    wo_hbm,
    out_ref,
    loc_ref,
    ct_ref,
    y_ref,
    z_ref,
    xs_ref,
    wo_ref,
    sems,
):
    moves = [
        (loc_hbm, loc_ref),
        (ct_hbm, ct_ref),
        (y_hbm, y_ref),
        (z_hbm, z_ref),
        (wo_hbm.at[layer], wo_ref),
        (xs_hbm, xs_ref),
    ]
    loads = [
        pltpu.make_async_copy(source, target, sems.at[k])
        for k, (source, target) in enumerate(moves)
    ]
    for load in loads:
        load.start()
    place = place_ref[0]
    decays = jnp.sum(recv_ref[:, 96:104, :].astype(F32), axis=1)
    source, between = iota((PEERS, PEERS), 0), iota((PEERS, PEERS), 1)
    if layer == 0:
        link = (between > place) & (between < source)
        valid = iota((PEERS, 128), 0) > place
    else:
        link = (between < place) & (between > source)
        valid = iota((PEERS, 128), 0) < place
    passed = dot(jnp.where(link, 1.0, 0.0), decays, EXACT)
    factor = jnp.where(valid, jnp.exp(passed), 0.0)
    mask = lax.shift_right_logical(iota((128, INNER), 1), 6) == iota((128, INNER), 0)
    factors = dot(factor, jnp.where(mask, 1.0, 0.0), EXACT)
    blocks = []
    for b in range(6):
        lanes = slice(128 * b, 128 * b + 128)
        total = jnp.zeros((16, 128), F32)
        for peer in range(PEERS):
            total = total + factors[peer : peer + 1, lanes] * recv_ref[
                peer, 16 * b : 16 * b + 16, :
            ].astype(F32)
        blocks.append(total)
    start = jnp.concatenate(blocks, axis=1)
    loads[0].wait()
    starts = [start, loc_ref[16:17, :] * start + loc_ref[0:16, :]]
    own = lax.shift_right_logical(iota((192, INNER), 1), 6) == lax.shift_right_logical(
        iota((192, INNER), 0), 4
    )
    mixed = []
    for load in loads[1:4]:
        load.wait()
    for g in range(2):
        span = slice(g * GROUP, (g + 1) * GROUP)
        wide = jnp.where(own, jnp.concatenate([starts[g]] * HEADS, axis=0), 0.0).astype(BF)
        y = y_ref[span, :] + dot(ct_ref[span, :], wide)
        gated = y * silu(z_ref[span, :].astype(F32))
        mixed.append(rms(gated, gain_ref[layer : layer + 1, :]).astype(BF))
    for load in loads[4:]:
        load.wait()
    result = (
        xs_ref[...].astype(F32) + dot(jnp.concatenate(mixed, axis=0), wo_ref[...])
    ).astype(BF)
    if layer == 1:
        out_ref[...] = result
        return
    row = iota((PEERS * CHUNK, 1), 0)
    peer = lax.shift_right_logical(row * 2731, 16)
    slot = row - CHUNK * peer
    token = (7 - jnp.bitwise_and(slot, 7)) * 64 + 63 - 2 * peer - lax.shift_right_logical(slot, 3)
    edge = (18 - slot) * 64 + 64 - 2 * peer
    token = jnp.where(slot < 16, token, jnp.where((slot < 19) & (peer > 0), edge, -1))
    out_ref[...] = (
        dot(one_hot((PEERS * CHUNK, TOKENS), token), result)
        .reshape(PEERS, CHUNK, D)
        .astype(BF)
    )


ANYWHERE = pl.BlockSpec(memory_space=pl.ANY)
VMEM = pl.BlockSpec(memory_space=pltpu.VMEM)


def shaped(shape, dtype):
    return jax.ShapeDtypeStruct(shape, dtype)


def kept(shape, dtype):
    return pltpu.HBM(shape, dtype)


def pinned(*arrays):
    return tuple(pltpu.with_memory_space_constraint(a, pltpu.HBM) for a in arrays)


def call(body, args, in_specs, outs, out_specs, scratch, flops, grid=()):
    moved = sum(a.size * a.dtype.itemsize for a in args) + sum(
        math.prod(o.shape) * jnp.dtype(o.dtype).itemsize for o in outs
    )
    return pl.pallas_call(
        body,
        grid=grid,
        out_shape=tuple(outs),
        in_specs=in_specs,
        out_specs=tuple(out_specs),
        scratch_shapes=scratch,
        compiler_params=pltpu.CompilerParams(vmem_limit_bytes=40 * 1024 * 1024),
        cost_estimate=pl.CostEstimate(flops=flops, bytes_accessed=moved, transcendentals=0),
    )(*args)


def whole(shape):
    return pl.BlockSpec(shape, lambda *_: (0,) * len(shape))


def exchange(chunks):
    return lax.all_to_all(chunks, "seq", 0, 0, tiled=True)


def front(layer, received, params):
    gain, in_weight, ws, conv_weight, conv_bias, cols, _, _, _ = params
    return call(
        functools.partial(front_body, layer),
        (received, gain, in_weight, ws, conv_weight, conv_bias, cols),
        [VMEM, VMEM, ANYWHERE, VMEM, VMEM, VMEM, VMEM],
        (
            kept((TOKENS, D), BF),
            kept((TOKENS, INNER), BF),
            kept((64, TOKENS), F32),
            kept((24, INNER), F32),
            kept((PEERS, STATE_ROWS, 128), BF),
        ),
        [ANYWHERE] * 5,
        [
            pltpu.VMEM((D, INNER), BF),
            pltpu.VMEM((TOKENS + 8, INNER), F32),
            pltpu.VMEM((TOKENS, D), BF),
            pltpu.VMEM((TOKENS, INNER), BF),
            pltpu.VMEM((64, TOKENS), F32),
            pltpu.VMEM((24, INNER), F32),
            pltpu.VMEM((STATE_ROWS, 128), BF),
            pltpu.SemaphoreType.DMA((5,)),
            pltpu.SemaphoreType.DMA((PEERS,)),
        ],
        1_000_000_000,
    )


def middle(layer, xs, xc, rows, params):
    gain, in_weight, _, _, _, _, skip, _, _ = params
    outs = (
        kept((TOKENS, INNER), BF),
        kept((TOKENS, INNER), F32),
        kept((TOKENS, 192), BF),
    )
    return call(
        functools.partial(middle_body, layer),
        (xs, gain, in_weight, xc, rows, skip),
        [
            whole(xs.shape),
            whole(gain.shape),
            pl.BlockSpec((1, D, INNER), lambda *_: (layer, 0, 0)),
            whole(xc.shape),
            whole(rows.shape),
            whole(skip.shape),
        ],
        outs,
        [whole(o.shape) for o in outs],
        [pltpu.VMEM((TOKENS, 16), F32)],
        1_000_000_000,
        (1,),
    )


def finish(layer, place, arrived, local, ct, y, z, xs, params):
    out_gain, out_weight = params[-2:]
    out = shaped((TOKENS, D), BF) if layer else shaped((PEERS, CHUNK, D), BF)
    return call(
        functools.partial(finish_body, layer),
        (place, arrived, local, ct, y, z, xs, out_gain, out_weight),
        [pl.BlockSpec(memory_space=pltpu.SMEM), VMEM] + [ANYWHERE] * 5 + [VMEM, ANYWHERE],
        (out,),
        [VMEM],
        [
            pltpu.VMEM((24, INNER), F32),
            pltpu.VMEM((TOKENS, 192), BF),
            pltpu.VMEM((TOKENS, INNER), F32),
            pltpu.VMEM((TOKENS, INNER), BF),
            pltpu.VMEM((TOKENS, D), BF),
            pltpu.VMEM((INNER, D), BF),
            pltpu.SemaphoreType.DMA((6,)),
        ],
        1_000_000_000,
    )[0]


def run_layer(layer, received, place, params):
    xs, xc, rows, local, send = pinned(*front(layer, received, params))
    arrived = pltpu.with_memory_space_constraint(exchange(send), pltpu.VMEM)
    z, y, ct = pinned(*middle(layer, xs, xc, rows, params))
    return finish(layer, place, arrived, local, ct, y, z, xs, params)


def on_device(
    slide_tiles,
    norm_gain,
    in_weight,
    state_weight,
    conv_weight,
    conv_bias,
    step_bias,
    decay_log,
    skip_gain,
    out_gain,
    out_weight,
):
    place = lax.axis_index("seq").astype(jnp.int32).reshape(1)
    ws = jnp.pad(jnp.swapaxes(state_weight, 1, 2), ((0, 0), (0, 4), (0, 0)))
    conv_cols = jnp.concatenate(
        [
            jnp.swapaxes(conv_weight[:, :, INNER:], 1, 2),
            conv_bias[:, INNER:, None],
            jnp.zeros((2, 32, 3), F32),
        ],
        axis=2,
    )
    head_cols = jnp.stack([step_bias, decay_log], axis=2)
    head_cols = jnp.pad(head_cols, ((0, 0), (0, 4), (5, 1)))
    cols = jnp.concatenate([conv_cols, head_cols], axis=1)
    skip = jnp.pad(skip_gain, ((0, 0), (0, 4)))
    slide_tiles, in_weight, out_weight = pinned(slide_tiles, in_weight, out_weight)
    params = (
        norm_gain,
        in_weight,
        ws,
        conv_weight,
        conv_bias,
        cols,
        skip,
        out_gain,
        out_weight,
    )
    (send,) = call(
        pack_body,
        (slide_tiles,),
        [ANYWHERE],
        (kept((PEERS, 56, 128), BF),),
        [ANYWHERE],
        [
            pltpu.VMEM(slide_tiles.shape, BF),
            pltpu.VMEM((PEERS, 56, 128), BF),
            pltpu.SemaphoreType.DMA((5,)),
        ],
        1_000_000,
    )
    between = run_layer(0, exchange(send), place, params)
    result = run_layer(1, exchange(between), place, params)
    return result.reshape(slide_tiles.shape)


def solution(mesh):
    placed = (P(("dp", "seq"), None, None), P(), P(), P(), P(), P(), P(), P(), P(), P(), P())
    return jax.shard_map(
        on_device,
        mesh=mesh,
        in_specs=placed,
        out_specs=P(("dp", "seq"), None, None),
        check_vma=False,
    )
```

```python
import functools
import math

import jax
import jax.numpy as jnp
from jax import lax
from jax.experimental import pallas as pl
from jax.experimental.pallas import tpu as pltpu
from jax.sharding import PartitionSpec as P

D = 384
INNER = 768
HEADS = 12
HEADDIM = 64
STATE = 16
GROUP = 256
TOKENS = 512
PEERS = 32
CHUNK = 24
STATE_ROWS = 104
WIDE = 256
EPS = 1e-05
BF = jnp.bfloat16
F32 = jnp.float32
EXACT = lax.Precision.HIGHEST


def iota(shape, dim):
    return lax.broadcasted_iota(jnp.int32, shape, dim)


def dot(a, b, precision=None):
    return lax.dot_general(
        a, b, (((1,), (0,)), ((), ())), precision=precision, preferred_element_type=F32
    )


def dot_rows(a, b):
    return lax.dot_general(a, b, (((1,), (1,)), ((), ())), preferred_element_type=F32)


def one_hot(shape, column):
    return jnp.where(iota(shape, 1) == column, 1.0, 0.0).astype(BF)


def silu(v):
    half = 0.5 * v
    return half + half * jnp.tanh(half)


def rms(values, gain):
    return values * lax.rsqrt(jnp.mean(values * values, axis=-1, keepdims=True) + EPS) * gain


def in_two(values):
    high = values.astype(BF)
    return high, (values - high.astype(F32)).astype(BF)


def spread(values, width):
    lanes = HEADS * width
    shift = width.bit_length() - 1
    mask = lax.shift_right_logical(iota((16, lanes), 1), shift) == iota((16, lanes), 0)
    return dot(values, jnp.where(mask, 1.0, 0.0), EXACT)


def pack_body(tiles_hbm, send_hbm, tiles_ref, send_ref, sems):
    load = pltpu.make_async_copy(tiles_hbm, tiles_ref, sems.at[0])
    load.start()
    load.wait()
    stores = []
    part = PEERS // 4
    slot = iota((part, 8, 128), 1)
    for q in range(4):
        halo = jnp.zeros((part, 8, 128), F32)
        for b in range(3):
            lanes = slice(128 * b, 128 * b + 128)
            first = 8 * part * q
            rows = [
                tiles_ref[r, first : first + 8 * part, lanes].astype(F32).reshape(part, 8, 128)
                for r in range(2)
            ]
            send_ref[part * q : part * q + part, 16 * b : 16 * b + 16, :] = jnp.concatenate(
                rows, axis=1
            ).astype(BF)
            for r in range(2):
                if q < 3:
                    beyond = tiles_ref[r, first + 8 * part : first + 8 * part + 16, lanes]
                    beyond = beyond.astype(F32)[0:1].reshape(1, 1, 128)
                else:
                    beyond = jnp.zeros((1, 1, 128), F32)
                after = jnp.concatenate([rows[r][1:, 0:1], beyond], axis=0)
                halo = jnp.where(slot == 2 * b + r, after, halo)
        send_ref[part * q : part * q + part, 48:56, :] = halo.astype(BF)
        own = pl.ds(part * q, part)
        store = pltpu.make_async_copy(send_ref.at[own], send_hbm.at[own], sems.at[1 + q])
        store.start()
        stores.append(store)
    for store in stores:
        store.wait()


def convolve(layer, normed, halo_normed, wx_ref, cw_ref, cb_ref, conv_ref, xc_ref):
    for first in range(0, INNER, WIDE):
        lanes = slice(first, first + WIDE)
        wx = wx_ref[:, lanes]
        conv_ref[8 : 8 + TOKENS, lanes] = dot(normed, wx).astype(BF).astype(F32)
        conv_ref[0:8, lanes] = dot(halo_normed, wx).astype(BF).astype(F32)[8:16]
    for first in range(0, INNER, 128):
        lanes = slice(first, first + 128)
        taps = 0.5 * cw_ref[layer, :, lanes]
        total = 0.5 * cb_ref[layer : layer + 1, lanes] + taps[0:1] * conv_ref[
            5 : 5 + TOKENS, lanes
        ]
        for tap in range(1, 4):
            total = total + taps[tap : tap + 1] * conv_ref[5 + tap : 5 + tap + TOKENS, lanes]
        xc_ref[:, lanes] = (total + total * jnp.tanh(total)).astype(BF)


def front_body(
    layer,
    recv_ref,
    gain_ref,
    wx_hbm,
    ws_ref,
    cw_ref,
    cb_ref,
    col_ref,
    xs_hbm,
    rows_hbm,
    loc_hbm,
    send_hbm,
    wx_ref,
    conv_ref,
    xs_ref,
    xc_ref,
    rows_ref,
    loc_ref,
    chunk_ref,
    all_ref,
    sems,
    send_sems,
):
    load = pltpu.make_async_copy(wx_hbm.at[layer, :, pl.ds(INNER, INNER)], wx_ref, sems.at[0])
    load.start()
    t = iota((TOKENS, 1), 0)
    place = iota((16, 1), 0)
    if layer == 0:
        main = jnp.concatenate(
            [recv_ref[:, 16 * b : 16 * b + 16, :].reshape(TOKENS, 128) for b in range(3)], axis=1
        )
        column = 511 - 8 * jnp.bitwise_and(t, 63) - lax.shift_right_logical(t, 6)
        halo_in = jnp.concatenate(
            [recv_ref[0, 48:56, :].astype(F32), recv_ref[1, 48:56, :].astype(F32)], axis=0
        ).astype(BF)
        picked = jnp.where(
            place == 13, 8, jnp.where(place == 14, 1, jnp.where(place == 15, 0, -16))
        )
        halo = jnp.concatenate(
            [dot(one_hot((16, 16), picked + 2 * b), halo_in) for b in range(3)], axis=1
        )
    else:
        main = recv_ref[:, 0:16, :].reshape(TOKENS, D)
        low = jnp.bitwise_and(t, 7)
        column = (
            2 * (jnp.bitwise_and(t, 255) - low) + 8 * lax.shift_right_logical(t, 8) + low
        )
        halo_in = jnp.concatenate(
            [recv_ref[PEERS - 1, 16:24, :].astype(F32), jnp.zeros((8, D), F32)], axis=0
        ).astype(BF)
        halo = dot(one_hot((16, 16), jnp.where(place >= 13, place - 13, -1)), halo_in)
    xs = dot(one_hot((TOKENS, TOKENS), column), main)
    xs_ref[0:TOKENS, :] = xs.astype(BF)
    xs_ref[TOKENS : TOKENS + 16, :] = halo.astype(BF)
    gain = gain_ref[layer : layer + 1, :]
    normed = rms(xs, gain).astype(BF)
    halo_normed = rms(halo, gain).astype(BF)
    load.wait()
    stores = [pltpu.make_async_copy(xs_ref, xs_hbm, sems.at[1])]
    stores[0].start()
    convolve(layer, normed, halo_normed, wx_ref, cw_ref, cb_ref, conv_ref, xc_ref)
    tall = jnp.concatenate([normed, jnp.zeros((112, D), BF), halo_normed], axis=0)
    proj = dot_rows(ws_ref[layer], tall).astype(BF).astype(F32)
    col = col_ref[layer]
    bc_in = proj[0:32, :]
    bc = col[0:32, 4:5] + col[0:32, 3:4] * bc_in
    for back in range(1, 4):
        bc = bc + col[0:32, 3 - back : 4 - back] * pltpu.roll(bc_in, back, 1)
    rows_ref[0:32, :] = silu(bc[:, 0:TOKENS]).astype(BF).astype(F32)
    raw = proj[32:48, 0:TOKENS] + col[32:48, 5:6]
    step = jnp.maximum(raw, 0.0) + jnp.log1p(jnp.exp(-jnp.abs(raw)))
    rate = -step * jnp.exp(col[32:48, 6:7])
    upper = jnp.where(iota((GROUP, GROUP), 0) <= iota((GROUP, GROUP), 1), 1.0, 0.0)
    cums = [dot(rate[:, g * GROUP : (g + 1) * GROUP], upper, EXACT) for g in range(2)]
    cum_rows = jnp.concatenate(cums, axis=1)
    rt = cum_rows - jnp.log(step)
    rows_ref[32:48, :] = rt
    rows_ref[48:64, :] = cum_rows
    ends = [jnp.broadcast_to(c[:, GROUP - 1 : GROUP], (16, 128)) for c in cums]
    ends = [e.T[0:1] for e in ends]
    totals = jnp.concatenate([ends[0], ends[1], jnp.zeros((6, 16), F32)], axis=0)
    decays = spread(jnp.exp(totals), HEADDIM)
    loc_ref[16:24, :] = decays
    tilted = []
    for g in range(2):
        span = slice(g * GROUP, (g + 1) * GROUP)
        tail = jnp.exp(cums[g][:, GROUP - 1 : GROUP] - rt[:, span])
        bt = rows_ref[0:16, span]
        tilted.append([(bt * tail[h : h + 1, :]).astype(BF) for h in range(HEADS)])
    total = totals[0:1] + totals[1:2]
    high, low = in_two(total)
    pad = jnp.zeros((1, 112), F32)
    chunk_ref[96:104, :] = jnp.concatenate(
        [
            jnp.concatenate([high.astype(F32), pad], axis=1),
            jnp.concatenate([low.astype(F32), pad], axis=1),
            jnp.zeros((6, 128), F32),
        ],
        axis=0,
    )

    head = lax.shift_right_logical(iota((16, WIDE), 1), 6)
    for q in range(INNER // WIDE):
        lanes = slice(WIDE * q, WIDE * q + WIDE)
        heads = WIDE // HEADDIM
        found = []
        for g in range(2):
            every = dot(
                jnp.concatenate(tilted[g][heads * q : heads * q + heads], axis=0),
                xc_ref[g * GROUP : (g + 1) * GROUP, lanes],
            )
            local = every[0:16]
            for h in range(1, heads):
                local = jnp.where(head == h, every[16 * h : 16 * h + 16], local)
            found.append(local)
        loc_ref[0:16, lanes] = found[0]
        final = decays[1:2, lanes] * found[0] + found[1]
        for b in range(WIDE // 128):
            slot = 16 * (WIDE // 128 * q + b)
            chunk_ref[slot : slot + 16, :] = final[:, 128 * b : 128 * b + 128]
    packed = chunk_ref[...].astype(BF)
    for peer in range(8):
        all_ref[peer] = packed
    for part in range(4):
        target = send_hbm.at[pl.ds(8 * part, 8)]
        stores.append(pltpu.make_async_copy(all_ref, target, send_sems.at[part]))
        stores[-1].start()
    late = ((rows_ref, rows_hbm), (loc_ref, loc_hbm))
    for k, (source, target) in enumerate(late):
        stores.append(pltpu.make_async_copy(source, target, sems.at[2 + k]))
        stores[-1].start()
    for store in stores:
        store.wait()


def middle_body(
    layer,
    xs_ref,
    gain_ref,
    w_ref,
    cw_ref,
    cb_ref,
    rows_ref,
    skip_ref,
    z_ref,
    y_ref,
    ct_ref,
    cum_ref,
    conv_ref,
    xc_ref,
):
    every = rms(xs_ref[...].astype(F32), gain_ref[layer : layer + 1, :]).astype(BF)
    normed, halo_normed = every[0:TOKENS], every[TOKENS : TOKENS + 16]
    wx_ref = w_ref.at[0, :, pl.ds(INNER, INNER)]
    convolve(layer, normed, halo_normed, wx_ref, cw_ref, cb_ref, conv_ref, xc_ref)
    z_ref[...] = dot(normed, w_ref[0, :, 0:INNER]).astype(BF)
    bt_ref = rows_ref[0:16, :].astype(BF)
    held = rows_ref[0:32, :].T[:, 16:32].astype(BF)
    cum_ref[...] = rows_ref[48:64, :].T
    mask = jnp.bitwise_and(iota((16, 192), 1), 15) == iota((16, 192), 0)
    repeated = dot(held, jnp.where(mask, 1.0, 0.0).astype(BF))
    ct_ref[...] = (repeated * spread(jnp.exp(cum_ref[...]), STATE)).astype(BF)
    skip = spread(jnp.broadcast_to(skip_ref[layer : layer + 1, :], (8, 16)), HEADDIM)
    half = GROUP // 2
    lower = iota((half, half), 0) >= iota((half, half), 1)
    left = iota((1, 128), 1) < HEADDIM
    for g in range(2):
        base = g * GROUP
        scores = dot(held[base : base + GROUP], bt_ref[:, base : base + GROUP])
        s00 = jnp.where(lower, scores[:half, :half], 0.0)
        s10 = scores[half:, :half]
        s11 = jnp.where(lower, scores[half:, half:], 0.0)
        for pair in range(HEADS // 2):
            lanes = slice(128 * pair, 128 * pair + 128)
            x = xc_ref[base : base + GROUP, lanes].astype(F32)
            top, low, inputs0, inputs1 = [], [], [], []
            for which in range(2):
                h = 2 * pair + which
                c0 = cum_ref[base : base + half, h : h + 1]
                c1 = cum_ref[base + half : base + GROUP, h : h + 1]
                r0 = rows_ref[32 + h : 33 + h, base : base + half]
                r1 = rows_ref[32 + h : 33 + h, base + half : base + GROUP]
                top.append((s00 * jnp.exp(jnp.minimum(c0 - r0, 80.0))).astype(BF))
                low.append((s10 * jnp.exp(c1 - r0)).astype(BF))
                low.append((s11 * jnp.exp(jnp.minimum(c1 - r1, 80.0))).astype(BF))
                own = jnp.where(left if which == 0 else ~left, x, 0.0).astype(BF)
                inputs0.append(own[:half])
                inputs1.append(own)
            y0 = dot(jnp.concatenate(top, axis=1), jnp.concatenate(inputs0, axis=0))
            y1 = dot(jnp.concatenate(low, axis=1), jnp.concatenate(inputs1, axis=0))
            weight = skip[0:1, lanes]
            y_ref[base : base + half, lanes] = y0 + weight * x[:half]
            y_ref[base + half : base + GROUP, lanes] = y1 + weight * x[half:]


def finish_body(
    layer,
    place_ref,
    recv_ref,
    loc_hbm,
    ct_hbm,
    y_hbm,
    z_hbm,
    xs_hbm,
    gain_ref,
    wo_hbm,
    out_ref,
    loc_ref,
    ct_ref,
    y_ref,
    z_ref,
    xs_ref,
    wo_ref,
    sems,
):
    moves = [
        (loc_hbm, loc_ref),
        (ct_hbm, ct_ref),
        (y_hbm, y_ref),
        (z_hbm, z_ref),
        (wo_hbm.at[layer], wo_ref),
        (xs_hbm.at[pl.ds(0, TOKENS)], xs_ref),
    ]
    loads = [
        pltpu.make_async_copy(source, target, sems.at[k])
        for k, (source, target) in enumerate(moves)
    ]
    for load in loads:
        load.start()
    place = place_ref[0]
    decays = jnp.sum(recv_ref[:, 96:104, :].astype(F32), axis=1)
    source, between = iota((PEERS, PEERS), 0), iota((PEERS, PEERS), 1)
    if layer == 0:
        link = (between > place) & (between < source)
        valid = iota((PEERS, 128), 0) > place
    else:
        link = (between < place) & (between > source)
        valid = iota((PEERS, 128), 0) < place
    passed = dot(jnp.where(link, 1.0, 0.0), decays, EXACT)
    factor = jnp.where(valid, jnp.exp(passed), 0.0)
    mask = lax.shift_right_logical(iota((128, INNER), 1), 6) == iota((128, INNER), 0)
    factors = dot(factor, jnp.where(mask, 1.0, 0.0), EXACT)
    blocks = []
    for b in range(6):
        lanes = slice(128 * b, 128 * b + 128)
        total = jnp.zeros((16, 128), F32)
        for peer in range(PEERS):
            total = total + factors[peer : peer + 1, lanes] * recv_ref[
                peer, 16 * b : 16 * b + 16, :
            ].astype(F32)
        blocks.append(total)
    start = jnp.concatenate(blocks, axis=1)
    loads[0].wait()
    starts = [start, loc_ref[16:17, :] * start + loc_ref[0:16, :]]
    own = lax.shift_right_logical(iota((192, INNER), 1), 6) == lax.shift_right_logical(
        iota((192, INNER), 0), 4
    )
    mixed = []
    for load in loads[1:4]:
        load.wait()
    for g in range(2):
        span = slice(g * GROUP, (g + 1) * GROUP)
        wide = jnp.where(own, jnp.concatenate([starts[g]] * HEADS, axis=0), 0.0).astype(BF)
        y = y_ref[span, :] + dot(ct_ref[span, :], wide)
        gated = y * silu(z_ref[span, :].astype(F32))
        mixed.append(rms(gated, gain_ref[layer : layer + 1, :]).astype(BF))
    for load in loads[4:]:
        load.wait()
    result = (
        xs_ref[...].astype(F32) + dot(jnp.concatenate(mixed, axis=0), wo_ref[...])
    ).astype(BF)
    if layer == 1:
        out_ref[...] = result
        return
    row = iota((PEERS * CHUNK, 1), 0)
    peer = lax.shift_right_logical(row * 2731, 16)
    slot = row - CHUNK * peer
    token = (7 - jnp.bitwise_and(slot, 7)) * 64 + 63 - 2 * peer - lax.shift_right_logical(slot, 3)
    edge = (18 - slot) * 64 + 64 - 2 * peer
    token = jnp.where(slot < 16, token, jnp.where((slot < 19) & (peer > 0), edge, -1))
    out_ref[...] = (
        dot(one_hot((PEERS * CHUNK, TOKENS), token), result)
        .reshape(PEERS, CHUNK, D)
        .astype(BF)
    )


ANYWHERE = pl.BlockSpec(memory_space=pl.ANY)
VMEM = pl.BlockSpec(memory_space=pltpu.VMEM)


def shaped(shape, dtype):
    return jax.ShapeDtypeStruct(shape, dtype)


def kept(shape, dtype):
    return pltpu.HBM(shape, dtype)


def pinned(*arrays):
    return tuple(pltpu.with_memory_space_constraint(a, pltpu.HBM) for a in arrays)


def call(body, args, in_specs, outs, out_specs, scratch, flops, grid=()):
    moved = sum(a.size * a.dtype.itemsize for a in args) + sum(
        math.prod(o.shape) * jnp.dtype(o.dtype).itemsize for o in outs
    )
    return pl.pallas_call(
        body,
        grid=grid,
        out_shape=tuple(outs),
        in_specs=in_specs,
        out_specs=tuple(out_specs),
        scratch_shapes=scratch,
        compiler_params=pltpu.CompilerParams(vmem_limit_bytes=40 * 1024 * 1024),
        cost_estimate=pl.CostEstimate(flops=flops, bytes_accessed=moved, transcendentals=0),
    )(*args)


def whole(shape):
    return pl.BlockSpec(shape, lambda *_: (0,) * len(shape))


def exchange(chunks):
    return lax.all_to_all(chunks, "seq", 0, 0, tiled=True)


def front(layer, received, params):
    gain, in_weight, ws, conv_weight, conv_bias, cols, _, _, _ = params
    return call(
        functools.partial(front_body, layer),
        (received, gain, in_weight, ws, conv_weight, conv_bias, cols),
        [VMEM, VMEM, ANYWHERE, VMEM, VMEM, VMEM, VMEM],
        (
            kept((TOKENS + 16, D), BF),
            kept((64, TOKENS), F32),
            kept((24, INNER), F32),
            kept((PEERS, STATE_ROWS, 128), BF),
        ),
        [ANYWHERE] * 4,
        [
            pltpu.VMEM((D, INNER), BF),
            pltpu.VMEM((TOKENS + 8, INNER), F32),
            pltpu.VMEM((TOKENS + 16, D), BF),
            pltpu.VMEM((TOKENS, INNER), BF),
            pltpu.VMEM((64, TOKENS), F32),
            pltpu.VMEM((24, INNER), F32),
            pltpu.VMEM((STATE_ROWS, 128), F32),
            pltpu.VMEM((8, STATE_ROWS, 128), BF),
            pltpu.SemaphoreType.DMA((4,)),
            pltpu.SemaphoreType.DMA((4,)),
        ],
        1_000_000_000,
    )


def middle(layer, xs, rows, params):
    gain, in_weight, _, conv_weight, conv_bias, _, skip, _, _ = params
    outs = (
        kept((TOKENS, INNER), BF),
        kept((TOKENS, INNER), F32),
        kept((TOKENS, 192), BF),
    )
    args = (xs, gain, in_weight, conv_weight, conv_bias, rows, skip)
    specs = [whole(a.shape) for a in args]
    specs[2] = pl.BlockSpec((1, D, 2 * INNER), lambda *_: (layer, 0, 0))
    return call(
        functools.partial(middle_body, layer),
        args,
        specs,
        outs,
        [whole(o.shape) for o in outs],
        [
            pltpu.VMEM((TOKENS, 16), F32),
            pltpu.VMEM((TOKENS + 8, INNER), F32),
            pltpu.VMEM((TOKENS, INNER), BF),
        ],
        1_000_000_000,
        (1,),
    )


def finish(layer, place, arrived, local, ct, y, z, xs, params):
    out_gain, out_weight = params[-2:]
    out = shaped((TOKENS, D), BF) if layer else shaped((PEERS, CHUNK, D), BF)
    return call(
        functools.partial(finish_body, layer),
        (place, arrived, local, ct, y, z, xs, out_gain, out_weight),
        [pl.BlockSpec(memory_space=pltpu.SMEM), VMEM] + [ANYWHERE] * 5 + [VMEM, ANYWHERE],
        (out,),
        [VMEM],
        [
            pltpu.VMEM((24, INNER), F32),
            pltpu.VMEM((TOKENS, 192), BF),
            pltpu.VMEM((TOKENS, INNER), F32),
            pltpu.VMEM((TOKENS, INNER), BF),
            pltpu.VMEM((TOKENS, D), BF),
            pltpu.VMEM((INNER, D), BF),
            pltpu.SemaphoreType.DMA((6,)),
        ],
        1_000_000_000,
    )[0]


def run_layer(layer, received, place, params):
    xs, rows, local, send = pinned(*front(layer, received, params))
    arrived = pltpu.with_memory_space_constraint(exchange(send), pltpu.VMEM)
    z, y, ct = pinned(*middle(layer, xs, rows, params))
    return finish(layer, place, arrived, local, ct, y, z, xs, params)


def on_device(
    slide_tiles,
    norm_gain,
    in_weight,
    state_weight,
    conv_weight,
    conv_bias,
    step_bias,
    decay_log,
    skip_gain,
    out_gain,
    out_weight,
):
    place = lax.axis_index("seq").astype(jnp.int32).reshape(1)
    ws = jnp.pad(jnp.swapaxes(state_weight, 1, 2), ((0, 0), (0, 4), (0, 0)))
    conv_cols = jnp.concatenate(
        [
            jnp.swapaxes(conv_weight[:, :, INNER:], 1, 2),
            conv_bias[:, INNER:, None],
            jnp.zeros((2, 32, 3), F32),
        ],
        axis=2,
    )
    head_cols = jnp.stack([step_bias, decay_log], axis=2)
    head_cols = jnp.pad(head_cols, ((0, 0), (0, 4), (5, 1)))
    cols = jnp.concatenate([conv_cols, head_cols], axis=1)
    skip = jnp.pad(skip_gain, ((0, 0), (0, 4)))
    slide_tiles, in_weight, out_weight = pinned(slide_tiles, in_weight, out_weight)
    params = (
        norm_gain,
        in_weight,
        ws,
        conv_weight,
        conv_bias,
        cols,
        skip,
        out_gain,
        out_weight,
    )
    (send,) = call(
        pack_body,
        (slide_tiles,),
        [ANYWHERE],
        (kept((PEERS, 56, 128), BF),),
        [ANYWHERE],
        [
            pltpu.VMEM(slide_tiles.shape, BF),
            pltpu.VMEM((PEERS, 56, 128), BF),
            pltpu.SemaphoreType.DMA((5,)),
        ],
        1_000_000,
    )
    between = run_layer(0, exchange(send), place, params)
    result = run_layer(1, exchange(between), place, params)
    return result.reshape(slide_tiles.shape)


def solution(mesh):
    placed = (P(("dp", "seq"), None, None), P(), P(), P(), P(), P(), P(), P(), P(), P(), P())
    return jax.shard_map(
        on_device,
        mesh=mesh,
        in_specs=placed,
        out_specs=P(("dp", "seq"), None, None),
        check_vma=False,
    )
```

```python
import functools
import math

import jax
import jax.numpy as jnp
from jax import lax
from jax.experimental import pallas as pl
from jax.experimental.pallas import tpu as pltpu
from jax.sharding import PartitionSpec as P

D = 384
INNER = 768
HEADS = 12
HEADDIM = 64
STATE = 16
GROUP = 256
TOKENS = 512
PEERS = 32
CHUNK = 24
STATE_ROWS = 104
WIDE = 256
EPS = 1e-05
BF = jnp.bfloat16
F32 = jnp.float32
EXACT = lax.Precision.HIGHEST


def iota(shape, dim):
    return lax.broadcasted_iota(jnp.int32, shape, dim)


def dot(a, b, precision=None):
    return lax.dot_general(
        a, b, (((1,), (0,)), ((), ())), precision=precision, preferred_element_type=F32
    )


def dot_rows(a, b):
    return lax.dot_general(a, b, (((1,), (1,)), ((), ())), preferred_element_type=F32)


def one_hot(shape, column):
    return jnp.where(iota(shape, 1) == column, 1.0, 0.0).astype(BF)


def silu(v):
    half = 0.5 * v
    return half + half * jnp.tanh(half)


def rms(values, gain):
    return values * lax.rsqrt(jnp.mean(values * values, axis=-1, keepdims=True) + EPS) * gain


def in_two(values):
    high = values.astype(BF)
    return high, (values - high.astype(F32)).astype(BF)


def spread(values, width):
    lanes = HEADS * width
    shift = width.bit_length() - 1
    mask = lax.shift_right_logical(iota((16, lanes), 1), shift) == iota((16, lanes), 0)
    return dot(values, jnp.where(mask, 1.0, 0.0), EXACT)


def pack_body(tiles_hbm, send_hbm, tiles_ref, send_ref, sems):
    part = PEERS // 4
    loads = []
    for q in range(4):
        own = pl.ds(8 * part * q, 8 * part)
        loads.append(
            pltpu.make_async_copy(tiles_hbm.at[:, own], tiles_ref.at[:, own], sems.at[4 + q])
        )
    for load in loads[::-1]:
        load.start()
    stores = []
    slot = iota((part, 8, 128), 1)
    for q in (3, 2, 1, 0):
        loads[q].wait()
        halo = jnp.zeros((part, 8, 128), F32)
        for b in range(3):
            lanes = slice(128 * b, 128 * b + 128)
            first = 8 * part * q
            rows = [
                tiles_ref[r, first : first + 8 * part, lanes].astype(F32).reshape(part, 8, 128)
                for r in range(2)
            ]
            send_ref[part * q : part * q + part, 16 * b : 16 * b + 16, :] = jnp.concatenate(
                rows, axis=1
            ).astype(BF)
            for r in range(2):
                if q < 3:
                    beyond = tiles_ref[r, first + 8 * part : first + 8 * part + 16, lanes]
                    beyond = beyond.astype(F32)[0:1].reshape(1, 1, 128)
                else:
                    beyond = jnp.zeros((1, 1, 128), F32)
                after = jnp.concatenate([rows[r][1:, 0:1], beyond], axis=0)
                halo = jnp.where(slot == 2 * b + r, after, halo)
        send_ref[part * q : part * q + part, 48:56, :] = halo.astype(BF)
        own = pl.ds(part * q, part)
        store = pltpu.make_async_copy(send_ref.at[own], send_hbm.at[own], sems.at[q])
        store.start()
        stores.append(store)
    for store in stores:
        store.wait()


def convolve(layer, normed, halo_normed, wx_ref, cw_ref, cb_ref, conv_ref, xc_ref):
    for first in range(0, INNER, WIDE):
        lanes = slice(first, first + WIDE)
        wx = wx_ref[:, lanes]
        conv_ref[8 : 8 + TOKENS, lanes] = dot(normed, wx).astype(BF).astype(F32)
        conv_ref[0:8, lanes] = dot(halo_normed, wx).astype(BF).astype(F32)[8:16]
    for first in range(0, INNER, 128):
        lanes = slice(first, first + 128)
        taps = 0.5 * cw_ref[layer, :, lanes]
        total = 0.5 * cb_ref[layer : layer + 1, lanes] + taps[0:1] * conv_ref[
            5 : 5 + TOKENS, lanes
        ]
        for tap in range(1, 4):
            total = total + taps[tap : tap + 1] * conv_ref[5 + tap : 5 + tap + TOKENS, lanes]
        xc_ref[:, lanes] = (total + total * jnp.tanh(total)).astype(BF)


def front_body(
    layer,
    recv_ref,
    gain_ref,
    wx_hbm,
    ws_ref,
    cw_ref,
    cb_ref,
    col_ref,
    xs_hbm,
    rows_hbm,
    loc_hbm,
    send_hbm,
    wx_ref,
    conv_ref,
    xs_ref,
    xc_ref,
    rows_ref,
    loc_ref,
    chunk_ref,
    all_ref,
    sems,
    send_sems,
):
    load = pltpu.make_async_copy(wx_hbm.at[layer, :, pl.ds(INNER, INNER)], wx_ref, sems.at[0])
    load.start()
    t = iota((TOKENS, 1), 0)
    place = iota((16, 1), 0)
    if layer == 0:
        main = jnp.concatenate(
            [recv_ref[:, 16 * b : 16 * b + 16, :].reshape(TOKENS, 128) for b in range(3)], axis=1
        )
        column = 511 - 8 * jnp.bitwise_and(t, 63) - lax.shift_right_logical(t, 6)
        halo_in = jnp.concatenate(
            [recv_ref[0, 48:56, :].astype(F32), recv_ref[1, 48:56, :].astype(F32)], axis=0
        ).astype(BF)
        picked = jnp.where(
            place == 13, 8, jnp.where(place == 14, 1, jnp.where(place == 15, 0, -16))
        )
        halo = jnp.concatenate(
            [dot(one_hot((16, 16), picked + 2 * b), halo_in) for b in range(3)], axis=1
        )
    else:
        main = recv_ref[:, 0:16, :].reshape(TOKENS, D)
        low = jnp.bitwise_and(t, 7)
        column = (
            2 * (jnp.bitwise_and(t, 255) - low) + 8 * lax.shift_right_logical(t, 8) + low
        )
        halo_in = jnp.concatenate(
            [recv_ref[PEERS - 1, 16:24, :].astype(F32), jnp.zeros((8, D), F32)], axis=0
        ).astype(BF)
        halo = dot(one_hot((16, 16), jnp.where(place >= 13, place - 13, -1)), halo_in)
    xs = dot(one_hot((TOKENS, TOKENS), column), main)
    xs_ref[0:TOKENS, :] = xs.astype(BF)
    xs_ref[TOKENS : TOKENS + 16, :] = halo.astype(BF)
    gain = gain_ref[layer : layer + 1, :]
    normed = rms(xs, gain).astype(BF)
    halo_normed = rms(halo, gain).astype(BF)
    load.wait()
    stores = [pltpu.make_async_copy(xs_ref, xs_hbm, sems.at[1])]
    stores[0].start()
    convolve(layer, normed, halo_normed, wx_ref, cw_ref, cb_ref, conv_ref, xc_ref)
    tall = jnp.concatenate([normed, jnp.zeros((112, D), BF), halo_normed], axis=0)
    proj = dot_rows(ws_ref[layer], tall).astype(BF).astype(F32)
    col = col_ref[layer]
    bc_in = proj[0:32, :]
    bc = col[0:32, 4:5] + col[0:32, 3:4] * bc_in
    for back in range(1, 4):
        bc = bc + col[0:32, 3 - back : 4 - back] * pltpu.roll(bc_in, back, 1)
    rows_ref[0:32, :] = silu(bc[:, 0:TOKENS]).astype(BF).astype(F32)
    raw = proj[32:48, 0:TOKENS] + col[32:48, 5:6]
    step = jnp.maximum(raw, 0.0) + jnp.log1p(jnp.exp(-jnp.abs(raw)))
    rate = -step * jnp.exp(col[32:48, 6:7])
    upper = jnp.where(iota((GROUP, GROUP), 0) <= iota((GROUP, GROUP), 1), 1.0, 0.0)
    cums = [dot(rate[:, g * GROUP : (g + 1) * GROUP], upper, EXACT) for g in range(2)]
    cum_rows = jnp.concatenate(cums, axis=1)
    rt = cum_rows - jnp.log(step)
    rows_ref[32:48, :] = rt
    rows_ref[48:64, :] = cum_rows
    ends = [jnp.broadcast_to(c[:, GROUP - 1 : GROUP], (16, 128)) for c in cums]
    ends = [e.T[0:1] for e in ends]
    totals = jnp.concatenate([ends[0], ends[1], jnp.zeros((6, 16), F32)], axis=0)
    decays = spread(jnp.exp(totals), HEADDIM)
    loc_ref[16:24, :] = decays
    tilted = []
    for g in range(2):
        span = slice(g * GROUP, (g + 1) * GROUP)
        tail = jnp.exp(cums[g][:, GROUP - 1 : GROUP] - rt[:, span])
        bt = rows_ref[0:16, span]
        tilted.append([(bt * tail[h : h + 1, :]).astype(BF) for h in range(HEADS)])
    total = totals[0:1] + totals[1:2]
    high, low = in_two(total)
    pad = jnp.zeros((1, 112), F32)
    chunk_ref[96:104, :] = jnp.concatenate(
        [
            jnp.concatenate([high.astype(F32), pad], axis=1),
            jnp.concatenate([low.astype(F32), pad], axis=1),
            jnp.zeros((6, 128), F32),
        ],
        axis=0,
    )

    head = lax.shift_right_logical(iota((16, WIDE), 1), 6)
    for q in range(INNER // WIDE):
        lanes = slice(WIDE * q, WIDE * q + WIDE)
        heads = WIDE // HEADDIM
        found = []
        for g in range(2):
            every = dot(
                jnp.concatenate(tilted[g][heads * q : heads * q + heads], axis=0),
                xc_ref[g * GROUP : (g + 1) * GROUP, lanes],
            )
            local = every[0:16]
            for h in range(1, heads):
                local = jnp.where(head == h, every[16 * h : 16 * h + 16], local)
            found.append(local)
        loc_ref[0:16, lanes] = found[0]
        final = decays[1:2, lanes] * found[0] + found[1]
        for b in range(WIDE // 128):
            slot = 16 * (WIDE // 128 * q + b)
            chunk_ref[slot : slot + 16, :] = final[:, 128 * b : 128 * b + 128]
    packed = chunk_ref[...].astype(BF)
    for peer in range(8):
        all_ref[peer] = packed
    for part in range(4):
        target = send_hbm.at[pl.ds(8 * part, 8)]
        stores.append(pltpu.make_async_copy(all_ref, target, send_sems.at[part]))
        stores[-1].start()
    late = ((rows_ref, rows_hbm), (loc_ref, loc_hbm))
    for k, (source, target) in enumerate(late):
        stores.append(pltpu.make_async_copy(source, target, sems.at[2 + k]))
        stores[-1].start()
    for store in stores:
        store.wait()


def middle_body(
    layer,
    xs_ref,
    gain_ref,
    w_ref,
    cw_ref,
    cb_ref,
    rows_ref,
    skip_ref,
    z_ref,
    y_ref,
    ct_ref,
    cum_ref,
    conv_ref,
    xc_ref,
):
    every = rms(xs_ref[...].astype(F32), gain_ref[layer : layer + 1, :]).astype(BF)
    normed, halo_normed = every[0:TOKENS], every[TOKENS : TOKENS + 16]
    wx_ref = w_ref.at[0, :, pl.ds(INNER, INNER)]
    convolve(layer, normed, halo_normed, wx_ref, cw_ref, cb_ref, conv_ref, xc_ref)
    z_ref[...] = dot(normed, w_ref[0, :, 0:INNER]).astype(BF)
    bt_ref = rows_ref[0:16, :].astype(BF)
    held = rows_ref[0:32, :].T[:, 16:32].astype(BF)
    cum_ref[...] = rows_ref[48:64, :].T
    mask = jnp.bitwise_and(iota((16, 192), 1), 15) == iota((16, 192), 0)
    repeated = dot(held, jnp.where(mask, 1.0, 0.0).astype(BF))
    ct_ref[...] = (repeated * spread(jnp.exp(cum_ref[...]), STATE)).astype(BF)
    skip = spread(jnp.broadcast_to(skip_ref[layer : layer + 1, :], (8, 16)), HEADDIM)
    half = GROUP // 2
    lower = iota((half, half), 0) >= iota((half, half), 1)
    left = iota((1, 128), 1) < HEADDIM
    for g in range(2):
        base = g * GROUP
        scores = dot(held[base : base + GROUP], bt_ref[:, base : base + GROUP])
        s00 = jnp.where(lower, scores[:half, :half], 0.0)
        s10 = scores[half:, :half]
        s11 = jnp.where(lower, scores[half:, half:], 0.0)
        for pair in range(HEADS // 2):
            lanes = slice(128 * pair, 128 * pair + 128)
            x = xc_ref[base : base + GROUP, lanes].astype(F32)
            top, low, inputs0, inputs1 = [], [], [], []
            for which in range(2):
                h = 2 * pair + which
                c0 = cum_ref[base : base + half, h : h + 1]
                c1 = cum_ref[base + half : base + GROUP, h : h + 1]
                r0 = rows_ref[32 + h : 33 + h, base : base + half]
                r1 = rows_ref[32 + h : 33 + h, base + half : base + GROUP]
                top.append((s00 * jnp.exp(jnp.minimum(c0 - r0, 80.0))).astype(BF))
                low.append((s10 * jnp.exp(c1 - r0)).astype(BF))
                low.append((s11 * jnp.exp(jnp.minimum(c1 - r1, 80.0))).astype(BF))
                own = jnp.where(left if which == 0 else ~left, x, 0.0).astype(BF)
                inputs0.append(own[:half])
                inputs1.append(own)
            y0 = dot(jnp.concatenate(top, axis=1), jnp.concatenate(inputs0, axis=0))
            y1 = dot(jnp.concatenate(low, axis=1), jnp.concatenate(inputs1, axis=0))
            weight = skip[0:1, lanes]
            y_ref[base : base + half, lanes] = y0 + weight * x[:half]
            y_ref[base + half : base + GROUP, lanes] = y1 + weight * x[half:]


def finish_body(
    layer,
    place_ref,
    recv_ref,
    loc_hbm,
    ct_hbm,
    y_hbm,
    z_hbm,
    xs_hbm,
    gain_ref,
    wo_hbm,
    out_ref,
    loc_ref,
    ct_ref,
    y_ref,
    z_ref,
    xs_ref,
    wo_ref,
    sems,
):
    spans = [pl.ds(0, GROUP), pl.ds(GROUP, GROUP)]
    moves = [(loc_hbm, loc_ref), (ct_hbm, ct_ref)]
    moves += [(y_hbm.at[spans[0]], y_ref.at[spans[0]]), (z_hbm.at[spans[0]], z_ref.at[spans[0]])]
    moves += [(wo_hbm.at[layer], wo_ref), (xs_hbm.at[pl.ds(0, TOKENS)], xs_ref)]
    moves += [(y_hbm.at[spans[1]], y_ref.at[spans[1]]), (z_hbm.at[spans[1]], z_ref.at[spans[1]])]
    loads = [
        pltpu.make_async_copy(source, target, sems.at[k])
        for k, (source, target) in enumerate(moves)
    ]
    for load in loads:
        load.start()
    place = place_ref[0]
    decays = jnp.sum(recv_ref[:, 96:104, :].astype(F32), axis=1)
    source, between = iota((PEERS, PEERS), 0), iota((PEERS, PEERS), 1)
    if layer == 0:
        link = (between > place) & (between < source)
        valid = iota((PEERS, 128), 0) > place
    else:
        link = (between < place) & (between > source)
        valid = iota((PEERS, 128), 0) < place
    passed = dot(jnp.where(link, 1.0, 0.0), decays, EXACT)
    factor = jnp.where(valid, jnp.exp(passed), 0.0)
    mask = lax.shift_right_logical(iota((128, INNER), 1), 6) == iota((128, INNER), 0)
    factors = dot(factor, jnp.where(mask, 1.0, 0.0), EXACT)
    blocks = []
    for b in range(6):
        lanes = slice(128 * b, 128 * b + 128)
        total = jnp.zeros((16, 128), F32)
        for peer in range(PEERS):
            total = total + factors[peer : peer + 1, lanes] * recv_ref[
                peer, 16 * b : 16 * b + 16, :
            ].astype(F32)
        blocks.append(total)
    start = jnp.concatenate(blocks, axis=1)
    loads[0].wait()
    starts = [start, loc_ref[16:17, :] * start + loc_ref[0:16, :]]
    own = lax.shift_right_logical(iota((192, INNER), 1), 6) == lax.shift_right_logical(
        iota((192, INNER), 0), 4
    )
    row = iota((PEERS * CHUNK, 1), 0)
    peer = lax.shift_right_logical(row * 2731, 16)
    slot = row - CHUNK * peer
    token = (7 - jnp.bitwise_and(slot, 7)) * 64 + 63 - 2 * peer - lax.shift_right_logical(slot, 3)
    edge = (18 - slot) * 64 + 64 - 2 * peer
    token = jnp.where(slot < 16, token, jnp.where((slot < 19) & (peer > 0), edge, -1))
    gain = gain_ref[layer : layer + 1, :]
    results = []
    for g in range(2):
        span = slice(g * GROUP, (g + 1) * GROUP)
        for load in loads[6:] if g else loads[1:6]:
            load.wait()
        wide = jnp.where(own, jnp.concatenate([starts[g]] * HEADS, axis=0), 0.0).astype(BF)
        y = y_ref[span, :] + dot(ct_ref[span, :], wide)
        gated = y * silu(z_ref[span, :].astype(F32))
        mixed = rms(gated, gain).astype(BF)
        result = (xs_ref[span, :].astype(F32) + dot(mixed, wo_ref[...])).astype(BF)
        if layer == 1:
            out_ref[span, :] = result
        results.append(result)
    if layer == 0:
        out_ref[...] = (
            dot(one_hot((PEERS * CHUNK, GROUP), token), results[0])
            + dot(one_hot((PEERS * CHUNK, GROUP), token - GROUP), results[1])
        ).reshape(PEERS, CHUNK, D).astype(BF)


ANYWHERE = pl.BlockSpec(memory_space=pl.ANY)
VMEM = pl.BlockSpec(memory_space=pltpu.VMEM)


def shaped(shape, dtype):
    return jax.ShapeDtypeStruct(shape, dtype)


def kept(shape, dtype):
    return pltpu.HBM(shape, dtype)


def pinned(*arrays):
    return tuple(pltpu.with_memory_space_constraint(a, pltpu.HBM) for a in arrays)


def call(body, args, in_specs, outs, out_specs, scratch, flops, grid=()):
    moved = sum(a.size * a.dtype.itemsize for a in args) + sum(
        math.prod(o.shape) * jnp.dtype(o.dtype).itemsize for o in outs
    )
    return pl.pallas_call(
        body,
        grid=grid,
        out_shape=tuple(outs),
        in_specs=in_specs,
        out_specs=tuple(out_specs),
        scratch_shapes=scratch,
        compiler_params=pltpu.CompilerParams(vmem_limit_bytes=40 * 1024 * 1024),
        cost_estimate=pl.CostEstimate(flops=flops, bytes_accessed=moved, transcendentals=0),
    )(*args)


def whole(shape):
    return pl.BlockSpec(shape, lambda *_: (0,) * len(shape))


def exchange(chunks):
    return lax.all_to_all(chunks, "seq", 0, 0, tiled=True)


def front(layer, received, params):
    gain, in_weight, ws, conv_weight, conv_bias, cols, _, _, _ = params
    return call(
        functools.partial(front_body, layer),
        (received, gain, in_weight, ws, conv_weight, conv_bias, cols),
        [VMEM, VMEM, ANYWHERE, VMEM, VMEM, VMEM, VMEM],
        (
            kept((TOKENS + 16, D), BF),
            kept((64, TOKENS), F32),
            kept((24, INNER), F32),
            kept((PEERS, STATE_ROWS, 128), BF),
        ),
        [ANYWHERE] * 4,
        [
            pltpu.VMEM((D, INNER), BF),
            pltpu.VMEM((TOKENS + 8, INNER), F32),
            pltpu.VMEM((TOKENS + 16, D), BF),
            pltpu.VMEM((TOKENS, INNER), BF),
            pltpu.VMEM((64, TOKENS), F32),
            pltpu.VMEM((24, INNER), F32),
            pltpu.VMEM((STATE_ROWS, 128), F32),
            pltpu.VMEM((8, STATE_ROWS, 128), BF),
            pltpu.SemaphoreType.DMA((4,)),
            pltpu.SemaphoreType.DMA((4,)),
        ],
        1_000_000_000,
    )


def middle(layer, xs, rows, params):
    gain, in_weight, _, conv_weight, conv_bias, _, skip, _, _ = params
    outs = (
        kept((TOKENS, INNER), BF),
        kept((TOKENS, INNER), F32),
        kept((TOKENS, 192), BF),
    )
    args = (xs, gain, in_weight, conv_weight, conv_bias, rows, skip)
    specs = [whole(a.shape) for a in args]
    specs[2] = pl.BlockSpec((1, D, 2 * INNER), lambda *_: (layer, 0, 0))
    return call(
        functools.partial(middle_body, layer),
        args,
        specs,
        outs,
        [whole(o.shape) for o in outs],
        [
            pltpu.VMEM((TOKENS, 16), F32),
            pltpu.VMEM((TOKENS + 8, INNER), F32),
            pltpu.VMEM((TOKENS, INNER), BF),
        ],
        1_000_000_000,
        (1,),
    )


def finish(layer, place, arrived, local, ct, y, z, xs, params):
    out_gain, out_weight = params[-2:]
    out = shaped((TOKENS, D), BF) if layer else shaped((PEERS, CHUNK, D), BF)
    return call(
        functools.partial(finish_body, layer),
        (place, arrived, local, ct, y, z, xs, out_gain, out_weight),
        [pl.BlockSpec(memory_space=pltpu.SMEM), VMEM] + [ANYWHERE] * 5 + [VMEM, ANYWHERE],
        (out,),
        [VMEM],
        [
            pltpu.VMEM((24, INNER), F32),
            pltpu.VMEM((TOKENS, 192), BF),
            pltpu.VMEM((TOKENS, INNER), F32),
            pltpu.VMEM((TOKENS, INNER), BF),
            pltpu.VMEM((TOKENS, D), BF),
            pltpu.VMEM((INNER, D), BF),
            pltpu.SemaphoreType.DMA((8,)),
        ],
        1_000_000_000,
    )[0]


def run_layer(layer, received, place, params):
    xs, rows, local, send = pinned(*front(layer, received, params))
    arrived = pltpu.with_memory_space_constraint(exchange(send), pltpu.VMEM)
    z, y, ct = pinned(*middle(layer, xs, rows, params))
    return finish(layer, place, arrived, local, ct, y, z, xs, params)


def on_device(
    slide_tiles,
    norm_gain,
    in_weight,
    state_weight,
    conv_weight,
    conv_bias,
    step_bias,
    decay_log,
    skip_gain,
    out_gain,
    out_weight,
):
    place = lax.axis_index("seq").astype(jnp.int32).reshape(1)
    ws = jnp.pad(jnp.swapaxes(state_weight, 1, 2), ((0, 0), (0, 4), (0, 0)))
    conv_cols = jnp.concatenate(
        [
            jnp.swapaxes(conv_weight[:, :, INNER:], 1, 2),
            conv_bias[:, INNER:, None],
            jnp.zeros((2, 32, 3), F32),
        ],
        axis=2,
    )
    head_cols = jnp.stack([step_bias, decay_log], axis=2)
    head_cols = jnp.pad(head_cols, ((0, 0), (0, 4), (5, 1)))
    cols = jnp.concatenate([conv_cols, head_cols], axis=1)
    skip = jnp.pad(skip_gain, ((0, 0), (0, 4)))
    slide_tiles, in_weight, out_weight = pinned(slide_tiles, in_weight, out_weight)
    params = (
        norm_gain,
        in_weight,
        ws,
        conv_weight,
        conv_bias,
        cols,
        skip,
        out_gain,
        out_weight,
    )
    (send,) = call(
        pack_body,
        (slide_tiles,),
        [ANYWHERE],
        (kept((PEERS, 56, 128), BF),),
        [ANYWHERE],
        [
            pltpu.VMEM(slide_tiles.shape, BF),
            pltpu.VMEM((PEERS, 56, 128), BF),
            pltpu.SemaphoreType.DMA((8,)),
        ],
        1_000_000,
    )
    between = run_layer(0, exchange(send), place, params)
    result = run_layer(1, exchange(between), place, params)
    return result.reshape(slide_tiles.shape)


def solution(mesh):
    placed = (P(("dp", "seq"), None, None), P(), P(), P(), P(), P(), P(), P(), P(), P(), P())
    return jax.shard_map(
        on_device,
        mesh=mesh,
        in_specs=placed,
        out_specs=P(("dp", "seq"), None, None),
        check_vma=False,
    )
```

```python
import functools
import math

import jax
import jax.numpy as jnp
from jax import lax
from jax.experimental import pallas as pl
from jax.experimental.pallas import tpu as pltpu
from jax.sharding import PartitionSpec as P

D = 384
INNER = 768
HEADS = 12
HEADDIM = 64
STATE = 16
GROUP = 256
TOKENS = 512
PEERS = 32
CHUNK = 64
STATE_ROWS = 104
WIDE = 256
EPS = 1e-05
BF = jnp.bfloat16
F32 = jnp.float32
EXACT = lax.Precision.HIGHEST


def iota(shape, dim):
    return lax.broadcasted_iota(jnp.int32, shape, dim)


def dot(a, b, precision=None):
    return lax.dot_general(
        a, b, (((1,), (0,)), ((), ())), precision=precision, preferred_element_type=F32
    )


def dot_rows(a, b):
    return lax.dot_general(a, b, (((1,), (1,)), ((), ())), preferred_element_type=F32)


def one_hot(shape, column):
    return jnp.where(iota(shape, 1) == column, 1.0, 0.0).astype(BF)


def silu(v):
    half = 0.5 * v
    return half + half * jnp.tanh(half)


def rms(values, gain):
    return values * lax.rsqrt(jnp.mean(values * values, axis=-1, keepdims=True) + EPS) * gain


def in_two(values):
    high = values.astype(BF)
    return high, (values - high.astype(F32)).astype(BF)


def spread(values, width):
    lanes = HEADS * width
    shift = width.bit_length() - 1
    mask = lax.shift_right_logical(iota((16, lanes), 1), shift) == iota((16, lanes), 0)
    return dot(values, jnp.where(mask, 1.0, 0.0), EXACT)


def pack_body(tiles_hbm, send_hbm, tiles_ref, send_ref, sems):
    part = PEERS // 4
    loads = []
    for q in range(4):
        own = pl.ds(8 * part * q, 8 * part)
        loads.append(
            pltpu.make_async_copy(tiles_hbm.at[:, own], tiles_ref.at[:, own], sems.at[4 + q])
        )
    for load in loads[::-1]:
        load.start()
    stores = []
    slot = iota((part, 8, 128), 1)
    for q in (3, 2, 1, 0):
        loads[q].wait()
        halo = jnp.zeros((part, 8, 128), F32)
        for b in range(3):
            lanes = slice(128 * b, 128 * b + 128)
            first = 8 * part * q
            rows = [
                tiles_ref[r, first : first + 8 * part, lanes].astype(F32).reshape(part, 8, 128)
                for r in range(2)
            ]
            send_ref[part * q : part * q + part, 16 * b : 16 * b + 16, :] = jnp.concatenate(
                rows, axis=1
            ).astype(BF)
            for r in range(2):
                if q < 3:
                    beyond = tiles_ref[r, first + 8 * part : first + 8 * part + 16, lanes]
                    beyond = beyond.astype(F32)[0:1].reshape(1, 1, 128)
                else:
                    beyond = jnp.zeros((1, 1, 128), F32)
                after = jnp.concatenate([rows[r][1:, 0:1], beyond], axis=0)
                halo = jnp.where(slot == 2 * b + r, after, halo)
        send_ref[part * q : part * q + part, 48:56, :] = halo.astype(BF)
        own = pl.ds(part * q, part)
        store = pltpu.make_async_copy(send_ref.at[own], send_hbm.at[own], sems.at[q])
        store.start()
        stores.append(store)
    for store in stores:
        store.wait()


def convolve(layer, normed, halo_normed, wx_ref, cw_ref, cb_ref, conv_ref, xc_ref):
    for first in range(0, INNER, WIDE):
        lanes = slice(first, first + WIDE)
        wx = wx_ref[:, lanes]
        conv_ref[8 : 8 + TOKENS, lanes] = dot(normed, wx).astype(BF).astype(F32)
        conv_ref[0:8, lanes] = dot(halo_normed, wx).astype(BF).astype(F32)[8:16]
    for first in range(0, INNER, 128):
        lanes = slice(first, first + 128)
        taps = 0.5 * cw_ref[layer, :, lanes]
        total = 0.5 * cb_ref[layer : layer + 1, lanes] + taps[0:1] * conv_ref[
            5 : 5 + TOKENS, lanes
        ]
        for tap in range(1, 4):
            total = total + taps[tap : tap + 1] * conv_ref[5 + tap : 5 + tap + TOKENS, lanes]
        xc_ref[:, lanes] = (total + total * jnp.tanh(total)).astype(BF)


def front_body(
    layer,
    recv_ref,
    gain_ref,
    wx_hbm,
    ws_ref,
    cw_ref,
    cb_ref,
    col_ref,
    xs_hbm,
    rows_hbm,
    loc_hbm,
    send_hbm,
    wx_ref,
    conv_ref,
    xs_ref,
    xc_ref,
    rows_ref,
    loc_ref,
    chunk_ref,
    all_ref,
    sems,
    send_sems,
):
    load = pltpu.make_async_copy(wx_hbm.at[layer, :, pl.ds(INNER, INNER)], wx_ref, sems.at[0])
    load.start()
    t = iota((TOKENS, 1), 0)
    place = iota((16, 1), 0)
    if layer == 0:
        main = jnp.concatenate(
            [recv_ref[:, 16 * b : 16 * b + 16, :].reshape(TOKENS, 128) for b in range(3)], axis=1
        )
        column = 511 - 8 * jnp.bitwise_and(t, 63) - lax.shift_right_logical(t, 6)
        halo_in = jnp.concatenate(
            [recv_ref[0, 48:56, :].astype(F32), recv_ref[1, 48:56, :].astype(F32)], axis=0
        ).astype(BF)
        picked = jnp.where(
            place == 13, 8, jnp.where(place == 14, 1, jnp.where(place == 15, 0, -16))
        )
        halo = jnp.concatenate(
            [dot(one_hot((16, 16), picked + 2 * b), halo_in) for b in range(3)], axis=1
        )
        xs = dot(one_hot((TOKENS, TOKENS), column), main)
    else:
        parts = [recv_ref[:, 16 * b : 16 * b + 16, :].astype(F32) for b in range(3)]
        parts = [p.reshape(PEERS, 2, 8, 128) for p in parts]
        xs = jnp.concatenate(
            [jnp.concatenate([p[:, r].reshape(256, 128) for p in parts], axis=1) for r in range(2)],
            axis=0,
        )
        halo_in = recv_ref[PEERS - 1, 48:64, :]
        picked = jnp.where(place >= 13, place - 13, -16)
        halo = jnp.concatenate(
            [dot(one_hot((16, 16), picked + 3 * b), halo_in) for b in range(3)], axis=1
        )
    xs_ref[0:TOKENS, :] = xs.astype(BF)
    xs_ref[TOKENS : TOKENS + 16, :] = halo.astype(BF)
    gain = gain_ref[layer : layer + 1, :]
    normed = rms(xs, gain).astype(BF)
    halo_normed = rms(halo, gain).astype(BF)
    load.wait()
    stores = [pltpu.make_async_copy(xs_ref, xs_hbm, sems.at[1])]
    stores[0].start()
    convolve(layer, normed, halo_normed, wx_ref, cw_ref, cb_ref, conv_ref, xc_ref)
    tall = jnp.concatenate([normed, jnp.zeros((112, D), BF), halo_normed], axis=0)
    proj = dot_rows(ws_ref[layer], tall).astype(BF).astype(F32)
    col = col_ref[layer]
    bc_in = proj[0:32, :]
    bc = col[0:32, 4:5] + col[0:32, 3:4] * bc_in
    for back in range(1, 4):
        bc = bc + col[0:32, 3 - back : 4 - back] * pltpu.roll(bc_in, back, 1)
    rows_ref[0:32, :] = silu(bc[:, 0:TOKENS]).astype(BF).astype(F32)
    raw = proj[32:48, 0:TOKENS] + col[32:48, 5:6]
    step = jnp.maximum(raw, 0.0) + jnp.log1p(jnp.exp(-jnp.abs(raw)))
    rate = -step * jnp.exp(col[32:48, 6:7])
    upper = jnp.where(iota((GROUP, GROUP), 0) <= iota((GROUP, GROUP), 1), 1.0, 0.0)
    cums = [dot(rate[:, g * GROUP : (g + 1) * GROUP], upper, EXACT) for g in range(2)]
    cum_rows = jnp.concatenate(cums, axis=1)
    rt = cum_rows - jnp.log(step)
    rows_ref[32:48, :] = rt
    rows_ref[48:64, :] = cum_rows
    ends = [jnp.broadcast_to(c[:, GROUP - 1 : GROUP], (16, 128)) for c in cums]
    ends = [e.T[0:1] for e in ends]
    totals = jnp.concatenate([ends[0], ends[1], jnp.zeros((6, 16), F32)], axis=0)
    decays = spread(jnp.exp(totals), HEADDIM)
    loc_ref[16:24, :] = decays
    tilted = []
    for g in range(2):
        span = slice(g * GROUP, (g + 1) * GROUP)
        tail = jnp.exp(cums[g][:, GROUP - 1 : GROUP] - rt[:, span])
        bt = rows_ref[0:16, span]
        tilted.append([(bt * tail[h : h + 1, :]).astype(BF) for h in range(HEADS)])
    total = totals[0:1] + totals[1:2]
    high, low = in_two(total)
    pad = jnp.zeros((1, 112), F32)
    chunk_ref[96:104, :] = jnp.concatenate(
        [
            jnp.concatenate([high.astype(F32), pad], axis=1),
            jnp.concatenate([low.astype(F32), pad], axis=1),
            jnp.zeros((6, 128), F32),
        ],
        axis=0,
    )

    head = lax.shift_right_logical(iota((16, WIDE), 1), 6)
    for q in range(INNER // WIDE):
        lanes = slice(WIDE * q, WIDE * q + WIDE)
        heads = WIDE // HEADDIM
        found = []
        for g in range(2):
            every = dot(
                jnp.concatenate(tilted[g][heads * q : heads * q + heads], axis=0),
                xc_ref[g * GROUP : (g + 1) * GROUP, lanes],
            )
            local = every[0:16]
            for h in range(1, heads):
                local = jnp.where(head == h, every[16 * h : 16 * h + 16], local)
            found.append(local)
        loc_ref[0:16, lanes] = found[0]
        final = decays[1:2, lanes] * found[0] + found[1]
        for b in range(WIDE // 128):
            slot = 16 * (WIDE // 128 * q + b)
            chunk_ref[slot : slot + 16, :] = final[:, 128 * b : 128 * b + 128]
    packed = chunk_ref[...].astype(BF)
    for peer in range(8):
        all_ref[peer] = packed
    for part in range(4):
        target = send_hbm.at[pl.ds(8 * part, 8)]
        stores.append(pltpu.make_async_copy(all_ref, target, send_sems.at[part]))
        stores[-1].start()
    late = ((rows_ref, rows_hbm), (loc_ref, loc_hbm))
    for k, (source, target) in enumerate(late):
        stores.append(pltpu.make_async_copy(source, target, sems.at[2 + k]))
        stores[-1].start()
    for store in stores:
        store.wait()


def middle_body(
    layer,
    xs_ref,
    gain_ref,
    w_ref,
    cw_ref,
    cb_ref,
    rows_ref,
    skip_ref,
    z_ref,
    y_ref,
    ct_ref,
    cum_ref,
    conv_ref,
    xc_ref,
):
    every = rms(xs_ref[...].astype(F32), gain_ref[layer : layer + 1, :]).astype(BF)
    normed, halo_normed = every[0:TOKENS], every[TOKENS : TOKENS + 16]
    wx_ref = w_ref.at[0, :, pl.ds(INNER, INNER)]
    convolve(layer, normed, halo_normed, wx_ref, cw_ref, cb_ref, conv_ref, xc_ref)
    z_ref[...] = dot(normed, w_ref[0, :, 0:INNER]).astype(BF)
    bt_ref = rows_ref[0:16, :].astype(BF)
    held = rows_ref[0:32, :].T[:, 16:32].astype(BF)
    cum_ref[...] = rows_ref[48:64, :].T
    mask = jnp.bitwise_and(iota((16, 192), 1), 15) == iota((16, 192), 0)
    repeated = dot(held, jnp.where(mask, 1.0, 0.0).astype(BF))
    ct_ref[...] = (repeated * spread(jnp.exp(cum_ref[...]), STATE)).astype(BF)
    skip = spread(jnp.broadcast_to(skip_ref[layer : layer + 1, :], (8, 16)), HEADDIM)
    half = GROUP // 2
    lower = iota((half, half), 0) >= iota((half, half), 1)
    left = iota((1, 128), 1) < HEADDIM
    for g in range(2):
        base = g * GROUP
        scores = dot(held[base : base + GROUP], bt_ref[:, base : base + GROUP])
        s00 = jnp.where(lower, scores[:half, :half], 0.0)
        s10 = scores[half:, :half]
        s11 = jnp.where(lower, scores[half:, half:], 0.0)
        for pair in range(HEADS // 2):
            lanes = slice(128 * pair, 128 * pair + 128)
            x = xc_ref[base : base + GROUP, lanes].astype(F32)
            top, low, inputs0, inputs1 = [], [], [], []
            for which in range(2):
                h = 2 * pair + which
                c0 = cum_ref[base : base + half, h : h + 1]
                c1 = cum_ref[base + half : base + GROUP, h : h + 1]
                r0 = rows_ref[32 + h : 33 + h, base : base + half]
                r1 = rows_ref[32 + h : 33 + h, base + half : base + GROUP]
                top.append((s00 * jnp.exp(jnp.minimum(c0 - r0, 80.0))).astype(BF))
                low.append((s10 * jnp.exp(c1 - r0)).astype(BF))
                low.append((s11 * jnp.exp(jnp.minimum(c1 - r1, 80.0))).astype(BF))
                own = jnp.where(left if which == 0 else ~left, x, 0.0).astype(BF)
                inputs0.append(own[:half])
                inputs1.append(own)
            y0 = dot(jnp.concatenate(top, axis=1), jnp.concatenate(inputs0, axis=0))
            y1 = dot(jnp.concatenate(low, axis=1), jnp.concatenate(inputs1, axis=0))
            weight = skip[0:1, lanes]
            y_ref[base : base + half, lanes] = y0 + weight * x[:half]
            y_ref[base + half : base + GROUP, lanes] = y1 + weight * x[half:]


def finish_body(
    layer,
    place_ref,
    recv_ref,
    loc_hbm,
    ct_hbm,
    y_hbm,
    z_hbm,
    xs_hbm,
    gain_ref,
    wo_hbm,
    out_ref,
    loc_ref,
    ct_ref,
    y_ref,
    z_ref,
    xs_ref,
    wo_ref,
    sems,
):
    spans = [pl.ds(0, GROUP), pl.ds(GROUP, GROUP)]
    moves = [(loc_hbm, loc_ref), (ct_hbm, ct_ref)]
    moves += [(y_hbm.at[spans[0]], y_ref.at[spans[0]]), (z_hbm.at[spans[0]], z_ref.at[spans[0]])]
    moves += [(wo_hbm.at[layer], wo_ref), (xs_hbm.at[pl.ds(0, TOKENS)], xs_ref)]
    moves += [(y_hbm.at[spans[1]], y_ref.at[spans[1]]), (z_hbm.at[spans[1]], z_ref.at[spans[1]])]
    loads = [
        pltpu.make_async_copy(source, target, sems.at[k])
        for k, (source, target) in enumerate(moves)
    ]
    for load in loads:
        load.start()
    place = place_ref[0]
    decays = jnp.sum(recv_ref[:, 96:104, :].astype(F32), axis=1)
    source, between = iota((PEERS, PEERS), 0), iota((PEERS, PEERS), 1)
    if layer == 0:
        link = (between > place) & (between < source)
        valid = iota((PEERS, 128), 0) > place
    else:
        link = (between < place) & (between > source)
        valid = iota((PEERS, 128), 0) < place
    passed = dot(jnp.where(link, 1.0, 0.0), decays, EXACT)
    factor = jnp.where(valid, jnp.exp(passed), 0.0)
    mask = lax.shift_right_logical(iota((128, INNER), 1), 6) == iota((128, INNER), 0)
    factors = dot(factor, jnp.where(mask, 1.0, 0.0), EXACT)
    blocks = []
    for b in range(6):
        lanes = slice(128 * b, 128 * b + 128)
        total = jnp.zeros((16, 128), F32)
        for peer in range(PEERS):
            total = total + factors[peer : peer + 1, lanes] * recv_ref[
                peer, 16 * b : 16 * b + 16, :
            ].astype(F32)
        blocks.append(total)
    start = jnp.concatenate(blocks, axis=1)
    loads[0].wait()
    starts = [start, loc_ref[16:17, :] * start + loc_ref[0:16, :]]
    own = lax.shift_right_logical(iota((192, INNER), 1), 6) == lax.shift_right_logical(
        iota((192, INNER), 0), 4
    )
    gain = gain_ref[layer : layer + 1, :]
    results = []
    for g in range(2):
        span = slice(g * GROUP, (g + 1) * GROUP)
        for load in loads[6:] if g else loads[1:6]:
            load.wait()
        wide = jnp.where(own, jnp.concatenate([starts[g]] * HEADS, axis=0), 0.0).astype(BF)
        y = y_ref[span, :] + dot(ct_ref[span, :], wide)
        gated = y * silu(z_ref[span, :].astype(F32))
        mixed = rms(gated, gain).astype(BF)
        result = (xs_ref[span, :].astype(F32) + dot(mixed, wo_ref[...])).astype(BF)
        if layer == 1:
            out_ref[span, :] = result
        results.append(result)
    if layer == 0:
        row = iota((TOKENS, 1), 0)
        peer, slot = lax.shift_right_logical(row, 4), jnp.bitwise_and(row, 15)
        token = (
            (7 - jnp.bitwise_and(slot, 7)) * 64 + 63 - 2 * peer - lax.shift_right_logical(slot, 3)
        )
        moved = dot(one_hot((TOKENS, GROUP), token), results[0]) + dot(
            one_hot((TOKENS, GROUP), token - GROUP), results[1]
        )
        block = lax.shift_right_logical(slot * 11, 5)
        edge = GROUP * block + (2 - slot + 3 * block) * 64 + 64 - 2 * peer
        edge = jnp.where((slot < 9) & (peer > 0), edge, -1)
        lanes = [slice(128 * b, 128 * b + 128) for b in range(3)]
        stacked = jnp.concatenate([results[0][:, own] for own in lanes], axis=0)
        edges = dot(one_hot((TOKENS, 3 * GROUP), edge), stacked)
        for b, part in enumerate([moved[:, own] for own in lanes] + [edges]):
            out_ref[:, 16 * b : 16 * b + 16, :] = part.reshape(PEERS, 16, 128).astype(BF)


ANYWHERE = pl.BlockSpec(memory_space=pl.ANY)
VMEM = pl.BlockSpec(memory_space=pltpu.VMEM)


def shaped(shape, dtype):
    return jax.ShapeDtypeStruct(shape, dtype)


def kept(shape, dtype):
    return pltpu.HBM(shape, dtype)


def pinned(*arrays):
    return tuple(pltpu.with_memory_space_constraint(a, pltpu.HBM) for a in arrays)


def call(body, args, in_specs, outs, out_specs, scratch, flops, grid=()):
    moved = sum(a.size * a.dtype.itemsize for a in args) + sum(
        math.prod(o.shape) * jnp.dtype(o.dtype).itemsize for o in outs
    )
    return pl.pallas_call(
        body,
        grid=grid,
        out_shape=tuple(outs),
        in_specs=in_specs,
        out_specs=tuple(out_specs),
        scratch_shapes=scratch,
        compiler_params=pltpu.CompilerParams(vmem_limit_bytes=40 * 1024 * 1024),
        cost_estimate=pl.CostEstimate(flops=flops, bytes_accessed=moved, transcendentals=0),
    )(*args)


def whole(shape):
    return pl.BlockSpec(shape, lambda *_: (0,) * len(shape))


def exchange(chunks):
    return lax.all_to_all(chunks, "seq", 0, 0, tiled=True)


def front(layer, received, params):
    gain, in_weight, ws, conv_weight, conv_bias, cols, _, _, _ = params
    return call(
        functools.partial(front_body, layer),
        (received, gain, in_weight, ws, conv_weight, conv_bias, cols),
        [VMEM, VMEM, ANYWHERE, VMEM, VMEM, VMEM, VMEM],
        (
            kept((TOKENS + 16, D), BF),
            kept((64, TOKENS), F32),
            kept((24, INNER), F32),
            kept((PEERS, STATE_ROWS, 128), BF),
        ),
        [ANYWHERE] * 4,
        [
            pltpu.VMEM((D, INNER), BF),
            pltpu.VMEM((TOKENS + 8, INNER), F32),
            pltpu.VMEM((TOKENS + 16, D), BF),
            pltpu.VMEM((TOKENS, INNER), BF),
            pltpu.VMEM((64, TOKENS), F32),
            pltpu.VMEM((24, INNER), F32),
            pltpu.VMEM((STATE_ROWS, 128), F32),
            pltpu.VMEM((8, STATE_ROWS, 128), BF),
            pltpu.SemaphoreType.DMA((4,)),
            pltpu.SemaphoreType.DMA((4,)),
        ],
        1_000_000_000,
    )


def middle(layer, xs, rows, params):
    gain, in_weight, _, conv_weight, conv_bias, _, skip, _, _ = params
    outs = (
        kept((TOKENS, INNER), BF),
        kept((TOKENS, INNER), F32),
        kept((TOKENS, 192), BF),
    )
    args = (xs, gain, in_weight, conv_weight, conv_bias, rows, skip)
    specs = [whole(a.shape) for a in args]
    specs[2] = pl.BlockSpec((1, D, 2 * INNER), lambda *_: (layer, 0, 0))
    return call(
        functools.partial(middle_body, layer),
        args,
        specs,
        outs,
        [whole(o.shape) for o in outs],
        [
            pltpu.VMEM((TOKENS, 16), F32),
            pltpu.VMEM((TOKENS + 8, INNER), F32),
            pltpu.VMEM((TOKENS, INNER), BF),
        ],
        1_000_000_000,
        (1,),
    )


def finish(layer, place, arrived, local, ct, y, z, xs, params):
    out_gain, out_weight = params[-2:]
    out = shaped((TOKENS, D), BF) if layer else shaped((PEERS, CHUNK, 128), BF)
    return call(
        functools.partial(finish_body, layer),
        (place, arrived, local, ct, y, z, xs, out_gain, out_weight),
        [pl.BlockSpec(memory_space=pltpu.SMEM), VMEM] + [ANYWHERE] * 5 + [VMEM, ANYWHERE],
        (out,),
        [VMEM],
        [
            pltpu.VMEM((24, INNER), F32),
            pltpu.VMEM((TOKENS, 192), BF),
            pltpu.VMEM((TOKENS, INNER), F32),
            pltpu.VMEM((TOKENS, INNER), BF),
            pltpu.VMEM((TOKENS, D), BF),
            pltpu.VMEM((INNER, D), BF),
            pltpu.SemaphoreType.DMA((8,)),
        ],
        1_000_000_000,
    )[0]


def run_layer(layer, received, place, params):
    xs, rows, local, send = pinned(*front(layer, received, params))
    arrived = pltpu.with_memory_space_constraint(exchange(send), pltpu.VMEM)
    z, y, ct = pinned(*middle(layer, xs, rows, params))
    return finish(layer, place, arrived, local, ct, y, z, xs, params)


def on_device(
    slide_tiles,
    norm_gain,
    in_weight,
    state_weight,
    conv_weight,
    conv_bias,
    step_bias,
    decay_log,
    skip_gain,
    out_gain,
    out_weight,
):
    place = lax.axis_index("seq").astype(jnp.int32).reshape(1)
    ws = jnp.pad(jnp.swapaxes(state_weight, 1, 2), ((0, 0), (0, 4), (0, 0)))
    conv_cols = jnp.concatenate(
        [
            jnp.swapaxes(conv_weight[:, :, INNER:], 1, 2),
            conv_bias[:, INNER:, None],
            jnp.zeros((2, 32, 3), F32),
        ],
        axis=2,
    )
    head_cols = jnp.stack([step_bias, decay_log], axis=2)
    head_cols = jnp.pad(head_cols, ((0, 0), (0, 4), (5, 1)))
    cols = jnp.concatenate([conv_cols, head_cols], axis=1)
    skip = jnp.pad(skip_gain, ((0, 0), (0, 4)))
    slide_tiles, in_weight, out_weight = pinned(slide_tiles, in_weight, out_weight)
    params = (
        norm_gain,
        in_weight,
        ws,
        conv_weight,
        conv_bias,
        cols,
        skip,
        out_gain,
        out_weight,
    )
    (send,) = call(
        pack_body,
        (slide_tiles,),
        [ANYWHERE],
        (kept((PEERS, 56, 128), BF),),
        [ANYWHERE],
        [
            pltpu.VMEM(slide_tiles.shape, BF),
            pltpu.VMEM((PEERS, 56, 128), BF),
            pltpu.SemaphoreType.DMA((8,)),
        ],
        1_000_000,
    )
    between = run_layer(0, exchange(send), place, params)
    result = run_layer(1, exchange(between), place, params)
    return result.reshape(slide_tiles.shape)


def solution(mesh):
    placed = (P(("dp", "seq"), None, None), P(), P(), P(), P(), P(), P(), P(), P(), P(), P())
    return jax.shard_map(
        on_device,
        mesh=mesh,
        in_specs=placed,
        out_specs=P(("dp", "seq"), None, None),
        check_vma=False,
    )
```

```python
import functools
import math

import jax
import jax.numpy as jnp
from jax import lax
from jax.experimental import pallas as pl
from jax.experimental.pallas import tpu as pltpu
from jax.sharding import PartitionSpec as P

D = 384
INNER = 768
HEADS = 12
HEADDIM = 64
STATE = 16
GROUP = 256
TOKENS = 512
PEERS = 32
CHUNK = 64
STATE_ROWS = 104
WIDE = 256
EPS = 1e-05
BF = jnp.bfloat16
F32 = jnp.float32
EXACT = lax.Precision.HIGHEST


def iota(shape, dim):
    return lax.broadcasted_iota(jnp.int32, shape, dim)


def dot(a, b, precision=None):
    return lax.dot_general(
        a, b, (((1,), (0,)), ((), ())), precision=precision, preferred_element_type=F32
    )


def dot_rows(a, b):
    return lax.dot_general(a, b, (((1,), (1,)), ((), ())), preferred_element_type=F32)


def one_hot(shape, column):
    return jnp.where(iota(shape, 1) == column, 1.0, 0.0).astype(BF)


def silu(v):
    half = 0.5 * v
    return half + half * jnp.tanh(half)


def rms(values, gain):
    return values * lax.rsqrt(jnp.mean(values * values, axis=-1, keepdims=True) + EPS) * gain


def in_two(values):
    high = values.astype(BF)
    return high, (values - high.astype(F32)).astype(BF)


def spread(values, width):
    lanes = HEADS * width
    shift = width.bit_length() - 1
    mask = lax.shift_right_logical(iota((16, lanes), 1), shift) == iota((16, lanes), 0)
    return dot(values, jnp.where(mask, 1.0, 0.0), EXACT)


def pack_body(tiles_hbm, send_hbm, tiles_ref, send_ref, sems):
    part = PEERS // 4
    loads = []
    for q in range(4):
        own = pl.ds(8 * part * q, 8 * part)
        loads.append(
            pltpu.make_async_copy(tiles_hbm.at[:, own], tiles_ref.at[:, own], sems.at[4 + q])
        )
    for load in loads[::-1]:
        load.start()
    stores = []
    slot = iota((part, 8, 128), 1)
    for q in (3, 2, 1, 0):
        loads[q].wait()
        halo = jnp.zeros((part, 8, 128), F32)
        for b in range(3):
            lanes = slice(128 * b, 128 * b + 128)
            first = 8 * part * q
            rows = [
                tiles_ref[r, first : first + 8 * part, lanes].astype(F32).reshape(part, 8, 128)
                for r in range(2)
            ]
            send_ref[part * q : part * q + part, 16 * b : 16 * b + 16, :] = jnp.concatenate(
                rows, axis=1
            ).astype(BF)
            for r in range(2):
                if q < 3:
                    beyond = tiles_ref[r, first + 8 * part : first + 8 * part + 16, lanes]
                    beyond = beyond.astype(F32)[0:1].reshape(1, 1, 128)
                else:
                    beyond = jnp.zeros((1, 1, 128), F32)
                after = jnp.concatenate([rows[r][1:, 0:1], beyond], axis=0)
                halo = jnp.where(slot == 2 * b + r, after, halo)
        send_ref[part * q : part * q + part, 48:56, :] = halo.astype(BF)
        own = pl.ds(part * q, part)
        store = pltpu.make_async_copy(send_ref.at[own], send_hbm.at[own], sems.at[q])
        store.start()
        stores.append(store)
    for store in stores:
        store.wait()


def convolve(layer, normed, halo_normed, wx_ref, cw_ref, cb_ref, conv_ref, xc_ref):
    for first in range(0, INNER, WIDE):
        lanes = slice(first, first + WIDE)
        wx = wx_ref[:, lanes]
        conv_ref[8 : 8 + TOKENS, lanes] = dot(normed, wx).astype(BF).astype(F32)
        conv_ref[0:8, lanes] = dot(halo_normed, wx).astype(BF).astype(F32)[8:16]
    for first in range(0, INNER, 128):
        lanes = slice(first, first + 128)
        taps = 0.5 * cw_ref[layer, :, lanes]
        bias = 0.5 * cb_ref[layer : layer + 1, lanes]
        rows = conv_ref[:, lanes]
        total = bias + taps[3:4] * rows[8:]
        for back in range(1, 4):
            total = total + taps[3 - back : 4 - back] * pltpu.roll(rows, back, 0)[8:]
        xc_ref[:, lanes] = (total + total * jnp.tanh(total)).astype(BF)


def front_body(
    layer,
    recv_ref,
    gain_ref,
    wx_hbm,
    ws_ref,
    cw_ref,
    cb_ref,
    col_ref,
    xs_hbm,
    rows_hbm,
    loc_hbm,
    send_hbm,
    wx_ref,
    conv_ref,
    xs_ref,
    xc_ref,
    rows_ref,
    loc_ref,
    chunk_ref,
    all_ref,
    sems,
    send_sems,
):
    load = pltpu.make_async_copy(wx_hbm.at[layer, :, pl.ds(INNER, INNER)], wx_ref, sems.at[0])
    load.start()
    t = iota((TOKENS, 1), 0)
    place = iota((16, 1), 0)
    if layer == 0:
        main = jnp.concatenate(
            [recv_ref[:, 16 * b : 16 * b + 16, :].reshape(TOKENS, 128) for b in range(3)], axis=1
        )
        column = 511 - 8 * jnp.bitwise_and(t, 63) - lax.shift_right_logical(t, 6)
        halo_in = jnp.concatenate(
            [recv_ref[0, 48:56, :].astype(F32), recv_ref[1, 48:56, :].astype(F32)], axis=0
        ).astype(BF)
        picked = jnp.where(
            place == 13, 8, jnp.where(place == 14, 1, jnp.where(place == 15, 0, -16))
        )
        halo = jnp.concatenate(
            [dot(one_hot((16, 16), picked + 2 * b), halo_in) for b in range(3)], axis=1
        )
        xs = dot(one_hot((TOKENS, TOKENS), column), main)
    else:
        parts = [recv_ref[:, 16 * b : 16 * b + 16, :].astype(F32) for b in range(3)]
        parts = [p.reshape(PEERS, 2, 8, 128) for p in parts]
        xs = jnp.concatenate(
            [jnp.concatenate([p[:, r].reshape(256, 128) for p in parts], axis=1) for r in range(2)],
            axis=0,
        )
        halo_in = recv_ref[PEERS - 1, 48:64, :]
        picked = jnp.where(place >= 13, place - 13, -16)
        halo = jnp.concatenate(
            [dot(one_hot((16, 16), picked + 3 * b), halo_in) for b in range(3)], axis=1
        )
    xs_ref[0:TOKENS, :] = xs.astype(BF)
    xs_ref[TOKENS : TOKENS + 16, :] = halo.astype(BF)
    gain = gain_ref[layer : layer + 1, :]
    normed = rms(xs, gain).astype(BF)
    halo_normed = rms(halo, gain).astype(BF)
    load.wait()
    stores = [pltpu.make_async_copy(xs_ref, xs_hbm, sems.at[1])]
    stores[0].start()
    convolve(layer, normed, halo_normed, wx_ref, cw_ref, cb_ref, conv_ref, xc_ref)
    tall = jnp.concatenate([normed, jnp.zeros((112, D), BF), halo_normed], axis=0)
    proj = dot_rows(ws_ref[layer], tall).astype(BF).astype(F32)
    col = col_ref[layer]
    bc_in = proj[0:32, :]
    bc = col[0:32, 4:5] + col[0:32, 3:4] * bc_in
    for back in range(1, 4):
        bc = bc + col[0:32, 3 - back : 4 - back] * pltpu.roll(bc_in, back, 1)
    rows_ref[0:32, :] = silu(bc[:, 0:TOKENS]).astype(BF).astype(F32)
    raw = proj[32:48, 0:TOKENS] + col[32:48, 5:6]
    step = jnp.maximum(raw, 0.0) + jnp.log1p(jnp.exp(-jnp.abs(raw)))
    rate = -step * jnp.exp(col[32:48, 6:7])
    upper = jnp.where(iota((GROUP, GROUP), 0) <= iota((GROUP, GROUP), 1), 1.0, 0.0)
    cums = [dot(rate[:, g * GROUP : (g + 1) * GROUP], upper, EXACT) for g in range(2)]
    cum_rows = jnp.concatenate(cums, axis=1)
    rt = cum_rows - jnp.log(step)
    rows_ref[32:48, :] = rt
    rows_ref[48:64, :] = cum_rows
    ends = [jnp.broadcast_to(c[:, GROUP - 1 : GROUP], (16, 128)) for c in cums]
    ends = [e.T[0:1] for e in ends]
    totals = jnp.concatenate([ends[0], ends[1], jnp.zeros((6, 16), F32)], axis=0)
    decays = spread(jnp.exp(totals), HEADDIM)
    loc_ref[16:24, :] = decays
    tilted = []
    for g in range(2):
        span = slice(g * GROUP, (g + 1) * GROUP)
        tail = jnp.exp(cums[g][:, GROUP - 1 : GROUP] - rt[:, span])
        bt = rows_ref[0:16, span]
        tilted.append([(bt * tail[h : h + 1, :]).astype(BF) for h in range(HEADS)])
    total = totals[0:1] + totals[1:2]
    high, low = in_two(total)
    pad = jnp.zeros((1, 112), F32)
    chunk_ref[96:104, :] = jnp.concatenate(
        [
            jnp.concatenate([high.astype(F32), pad], axis=1),
            jnp.concatenate([low.astype(F32), pad], axis=1),
            jnp.zeros((6, 128), F32),
        ],
        axis=0,
    )

    head = lax.shift_right_logical(iota((16, WIDE), 1), 6)
    for q in range(INNER // WIDE):
        lanes = slice(WIDE * q, WIDE * q + WIDE)
        heads = WIDE // HEADDIM
        found = []
        for g in range(2):
            every = dot(
                jnp.concatenate(tilted[g][heads * q : heads * q + heads], axis=0),
                xc_ref[g * GROUP : (g + 1) * GROUP, lanes],
            )
            local = every[0:16]
            for h in range(1, heads):
                local = jnp.where(head == h, every[16 * h : 16 * h + 16], local)
            found.append(local)
        loc_ref[0:16, lanes] = found[0]
        final = decays[1:2, lanes] * found[0] + found[1]
        for b in range(WIDE // 128):
            slot = 16 * (WIDE // 128 * q + b)
            chunk_ref[slot : slot + 16, :] = final[:, 128 * b : 128 * b + 128]
    packed = chunk_ref[...].astype(BF)
    for peer in range(8):
        all_ref[peer] = packed
    for part in range(4):
        target = send_hbm.at[pl.ds(8 * part, 8)]
        stores.append(pltpu.make_async_copy(all_ref, target, send_sems.at[part]))
        stores[-1].start()
    late = ((rows_ref, rows_hbm), (loc_ref, loc_hbm))
    for k, (source, target) in enumerate(late):
        stores.append(pltpu.make_async_copy(source, target, sems.at[2 + k]))
        stores[-1].start()
    for store in stores:
        store.wait()


def middle_body(
    layer,
    xs_ref,
    gain_ref,
    w_ref,
    cw_ref,
    cb_ref,
    rows_ref,
    skip_ref,
    z_ref,
    y_ref,
    ct_ref,
    cum_ref,
    conv_ref,
    xc_ref,
):
    every = rms(xs_ref[...].astype(F32), gain_ref[layer : layer + 1, :]).astype(BF)
    normed, halo_normed = every[0:TOKENS], every[TOKENS : TOKENS + 16]
    wx_ref = w_ref.at[0, :, pl.ds(INNER, INNER)]
    convolve(layer, normed, halo_normed, wx_ref, cw_ref, cb_ref, conv_ref, xc_ref)
    z_ref[...] = dot(normed, w_ref[0, :, 0:INNER]).astype(BF)
    bt_ref = rows_ref[0:16, :].astype(BF)
    held = rows_ref[0:32, :].T[:, 16:32].astype(BF)
    cum_ref[...] = rows_ref[48:64, :].T
    mask = jnp.bitwise_and(iota((16, 192), 1), 15) == iota((16, 192), 0)
    repeated = dot(held, jnp.where(mask, 1.0, 0.0).astype(BF))
    ct_ref[...] = (repeated * spread(jnp.exp(cum_ref[...]), STATE)).astype(BF)
    skip = spread(jnp.broadcast_to(skip_ref[layer : layer + 1, :], (8, 16)), HEADDIM)
    half = GROUP // 2
    lower = iota((half, half), 0) >= iota((half, half), 1)
    left = iota((1, 128), 1) < HEADDIM
    for g in range(2):
        base = g * GROUP
        scores = dot(held[base : base + GROUP], bt_ref[:, base : base + GROUP])
        s00 = jnp.where(lower, scores[:half, :half], 0.0)
        s10 = scores[half:, :half]
        s11 = jnp.where(lower, scores[half:, half:], 0.0)
        for pair in range(HEADS // 2):
            lanes = slice(128 * pair, 128 * pair + 128)
            x = xc_ref[base : base + GROUP, lanes].astype(F32)
            top, low, inputs0, inputs1 = [], [], [], []
            for which in range(2):
                h = 2 * pair + which
                c0 = cum_ref[base : base + half, h : h + 1]
                c1 = cum_ref[base + half : base + GROUP, h : h + 1]
                r0 = rows_ref[32 + h : 33 + h, base : base + half]
                r1 = rows_ref[32 + h : 33 + h, base + half : base + GROUP]
                top.append((s00 * jnp.exp(jnp.minimum(c0 - r0, 80.0))).astype(BF))
                low.append((s10 * jnp.exp(c1 - r0)).astype(BF))
                low.append((s11 * jnp.exp(jnp.minimum(c1 - r1, 80.0))).astype(BF))
                own = jnp.where(left if which == 0 else ~left, x, 0.0).astype(BF)
                inputs0.append(own[:half])
                inputs1.append(own)
            y0 = dot(jnp.concatenate(top, axis=1), jnp.concatenate(inputs0, axis=0))
            y1 = dot(jnp.concatenate(low, axis=1), jnp.concatenate(inputs1, axis=0))
            weight = skip[0:1, lanes]
            y_ref[base : base + half, lanes] = y0 + weight * x[:half]
            y_ref[base + half : base + GROUP, lanes] = y1 + weight * x[half:]


def finish_body(
    layer,
    place_ref,
    recv_ref,
    loc_hbm,
    ct_hbm,
    y_hbm,
    z_hbm,
    xs_hbm,
    gain_ref,
    wo_hbm,
    out_ref,
    loc_ref,
    ct_ref,
    y_ref,
    z_ref,
    xs_ref,
    wo_ref,
    sems,
):
    spans = [pl.ds(0, GROUP), pl.ds(GROUP, GROUP)]
    moves = [(loc_hbm, loc_ref), (ct_hbm, ct_ref)]
    moves += [(y_hbm.at[spans[0]], y_ref.at[spans[0]]), (z_hbm.at[spans[0]], z_ref.at[spans[0]])]
    moves += [(wo_hbm.at[layer], wo_ref), (xs_hbm.at[pl.ds(0, TOKENS)], xs_ref)]
    moves += [(y_hbm.at[spans[1]], y_ref.at[spans[1]]), (z_hbm.at[spans[1]], z_ref.at[spans[1]])]
    loads = [
        pltpu.make_async_copy(source, target, sems.at[k])
        for k, (source, target) in enumerate(moves)
    ]
    for load in loads:
        load.start()
    place = place_ref[0]
    decays = jnp.sum(recv_ref[:, 96:104, :].astype(F32), axis=1)
    source, between = iota((PEERS, PEERS), 0), iota((PEERS, PEERS), 1)
    if layer == 0:
        link = (between > place) & (between < source)
        valid = iota((PEERS, 128), 0) > place
    else:
        link = (between < place) & (between > source)
        valid = iota((PEERS, 128), 0) < place
    passed = dot(jnp.where(link, 1.0, 0.0), decays, EXACT)
    factor = jnp.where(valid, jnp.exp(passed), 0.0)
    mask = lax.shift_right_logical(iota((128, INNER), 1), 6) == iota((128, INNER), 0)
    factors = dot(factor, jnp.where(mask, 1.0, 0.0), EXACT)
    blocks = []
    for b in range(6):
        lanes = slice(128 * b, 128 * b + 128)
        total = jnp.zeros((16, 128), F32)
        for peer in range(PEERS):
            total = total + factors[peer : peer + 1, lanes] * recv_ref[
                peer, 16 * b : 16 * b + 16, :
            ].astype(F32)
        blocks.append(total)
    start = jnp.concatenate(blocks, axis=1)
    loads[0].wait()
    starts = [start, loc_ref[16:17, :] * start + loc_ref[0:16, :]]
    own = lax.shift_right_logical(iota((192, INNER), 1), 6) == lax.shift_right_logical(
        iota((192, INNER), 0), 4
    )
    gain = gain_ref[layer : layer + 1, :]
    results = []
    for g in range(2):
        span = slice(g * GROUP, (g + 1) * GROUP)
        for load in loads[6:] if g else loads[1:6]:
            load.wait()
        wide = jnp.where(own, jnp.concatenate([starts[g]] * HEADS, axis=0), 0.0).astype(BF)
        y = y_ref[span, :] + dot(ct_ref[span, :], wide)
        gated = y * silu(z_ref[span, :].astype(F32))
        mixed = rms(gated, gain).astype(BF)
        result = (xs_ref[span, :].astype(F32) + dot(mixed, wo_ref[...])).astype(BF)
        if layer == 1:
            out_ref[span, :] = result
        results.append(result)
    if layer == 0:
        row = iota((TOKENS, 1), 0)
        peer, slot = lax.shift_right_logical(row, 4), jnp.bitwise_and(row, 15)
        token = (
            (7 - jnp.bitwise_and(slot, 7)) * 64 + 63 - 2 * peer - lax.shift_right_logical(slot, 3)
        )
        moved = dot(one_hot((TOKENS, GROUP), token), results[0]) + dot(
            one_hot((TOKENS, GROUP), token - GROUP), results[1]
        )
        block = lax.shift_right_logical(slot * 11, 5)
        edge = GROUP * block + (2 - slot + 3 * block) * 64 + 64 - 2 * peer
        edge = jnp.where((slot < 9) & (peer > 0), edge, -1)
        lanes = [slice(128 * b, 128 * b + 128) for b in range(3)]
        stacked = jnp.concatenate([results[0][:, own] for own in lanes], axis=0)
        edges = dot(one_hot((TOKENS, 3 * GROUP), edge), stacked)
        for b, part in enumerate([moved[:, own] for own in lanes] + [edges]):
            out_ref[:, 16 * b : 16 * b + 16, :] = part.reshape(PEERS, 16, 128).astype(BF)


ANYWHERE = pl.BlockSpec(memory_space=pl.ANY)
VMEM = pl.BlockSpec(memory_space=pltpu.VMEM)


def shaped(shape, dtype):
    return jax.ShapeDtypeStruct(shape, dtype)


def kept(shape, dtype):
    return pltpu.HBM(shape, dtype)


def pinned(*arrays):
    return tuple(pltpu.with_memory_space_constraint(a, pltpu.HBM) for a in arrays)


def call(body, args, in_specs, outs, out_specs, scratch, flops, grid=()):
    moved = sum(a.size * a.dtype.itemsize for a in args) + sum(
        math.prod(o.shape) * jnp.dtype(o.dtype).itemsize for o in outs
    )
    return pl.pallas_call(
        body,
        grid=grid,
        out_shape=tuple(outs),
        in_specs=in_specs,
        out_specs=tuple(out_specs),
        scratch_shapes=scratch,
        compiler_params=pltpu.CompilerParams(vmem_limit_bytes=40 * 1024 * 1024),
        cost_estimate=pl.CostEstimate(flops=flops, bytes_accessed=moved, transcendentals=0),
    )(*args)


def whole(shape):
    return pl.BlockSpec(shape, lambda *_: (0,) * len(shape))


def exchange(chunks):
    return lax.all_to_all(chunks, "seq", 0, 0, tiled=True)


def front(layer, received, params):
    gain, in_weight, ws, conv_weight, conv_bias, cols, _, _, _ = params
    return call(
        functools.partial(front_body, layer),
        (received, gain, in_weight, ws, conv_weight, conv_bias, cols),
        [VMEM, VMEM, ANYWHERE, VMEM, VMEM, VMEM, VMEM],
        (
            kept((TOKENS + 16, D), BF),
            kept((64, TOKENS), F32),
            kept((24, INNER), F32),
            kept((PEERS, STATE_ROWS, 128), BF),
        ),
        [ANYWHERE] * 4,
        [
            pltpu.VMEM((D, INNER), BF),
            pltpu.VMEM((TOKENS + 8, INNER), F32),
            pltpu.VMEM((TOKENS + 16, D), BF),
            pltpu.VMEM((TOKENS, INNER), BF),
            pltpu.VMEM((64, TOKENS), F32),
            pltpu.VMEM((24, INNER), F32),
            pltpu.VMEM((STATE_ROWS, 128), F32),
            pltpu.VMEM((8, STATE_ROWS, 128), BF),
            pltpu.SemaphoreType.DMA((4,)),
            pltpu.SemaphoreType.DMA((4,)),
        ],
        1_000_000_000,
    )


def middle(layer, xs, rows, params):
    gain, in_weight, _, conv_weight, conv_bias, _, skip, _, _ = params
    outs = (
        kept((TOKENS, INNER), BF),
        kept((TOKENS, INNER), F32),
        kept((TOKENS, 192), BF),
    )
    args = (xs, gain, in_weight, conv_weight, conv_bias, rows, skip)
    specs = [whole(a.shape) for a in args]
    specs[2] = pl.BlockSpec((1, D, 2 * INNER), lambda *_: (layer, 0, 0))
    return call(
        functools.partial(middle_body, layer),
        args,
        specs,
        outs,
        [whole(o.shape) for o in outs],
        [
            pltpu.VMEM((TOKENS, 16), F32),
            pltpu.VMEM((TOKENS + 8, INNER), F32),
            pltpu.VMEM((TOKENS, INNER), BF),
        ],
        1_000_000_000,
        (1,),
    )


def finish(layer, place, arrived, local, ct, y, z, xs, params):
    out_gain, out_weight = params[-2:]
    out = shaped((TOKENS, D), BF) if layer else shaped((PEERS, CHUNK, 128), BF)
    return call(
        functools.partial(finish_body, layer),
        (place, arrived, local, ct, y, z, xs, out_gain, out_weight),
        [pl.BlockSpec(memory_space=pltpu.SMEM), VMEM] + [ANYWHERE] * 5 + [VMEM, ANYWHERE],
        (out,),
        [VMEM],
        [
            pltpu.VMEM((24, INNER), F32),
            pltpu.VMEM((TOKENS, 192), BF),
            pltpu.VMEM((TOKENS, INNER), F32),
            pltpu.VMEM((TOKENS, INNER), BF),
            pltpu.VMEM((TOKENS, D), BF),
            pltpu.VMEM((INNER, D), BF),
            pltpu.SemaphoreType.DMA((8,)),
        ],
        1_000_000_000,
    )[0]


def run_layer(layer, received, place, params):
    xs, rows, local, send = pinned(*front(layer, received, params))
    arrived = pltpu.with_memory_space_constraint(exchange(send), pltpu.VMEM)
    z, y, ct = pinned(*middle(layer, xs, rows, params))
    return finish(layer, place, arrived, local, ct, y, z, xs, params)


def on_device(
    slide_tiles,
    norm_gain,
    in_weight,
    state_weight,
    conv_weight,
    conv_bias,
    step_bias,
    decay_log,
    skip_gain,
    out_gain,
    out_weight,
):
    place = lax.axis_index("seq").astype(jnp.int32).reshape(1)
    ws = jnp.pad(jnp.swapaxes(state_weight, 1, 2), ((0, 0), (0, 4), (0, 0)))
    conv_cols = jnp.concatenate(
        [
            jnp.swapaxes(conv_weight[:, :, INNER:], 1, 2),
            conv_bias[:, INNER:, None],
            jnp.zeros((2, 32, 3), F32),
        ],
        axis=2,
    )
    head_cols = jnp.stack([step_bias, decay_log], axis=2)
    head_cols = jnp.pad(head_cols, ((0, 0), (0, 4), (5, 1)))
    cols = jnp.concatenate([conv_cols, head_cols], axis=1)
    skip = jnp.pad(skip_gain, ((0, 0), (0, 4)))
    slide_tiles, in_weight, out_weight = pinned(slide_tiles, in_weight, out_weight)
    params = (
        norm_gain,
        in_weight,
        ws,
        conv_weight,
        conv_bias,
        cols,
        skip,
        out_gain,
        out_weight,
    )
    (send,) = call(
        pack_body,
        (slide_tiles,),
        [ANYWHERE],
        (kept((PEERS, 56, 128), BF),),
        [ANYWHERE],
        [
            pltpu.VMEM(slide_tiles.shape, BF),
            pltpu.VMEM((PEERS, 56, 128), BF),
            pltpu.SemaphoreType.DMA((8,)),
        ],
        1_000_000,
    )
    between = run_layer(0, exchange(send), place, params)
    result = run_layer(1, exchange(between), place, params)
    return result.reshape(slide_tiles.shape)


def solution(mesh):
    placed = (P(("dp", "seq"), None, None), P(), P(), P(), P(), P(), P(), P(), P(), P(), P())
    return jax.shard_map(
        on_device,
        mesh=mesh,
        in_specs=placed,
        out_specs=P(("dp", "seq"), None, None),
        check_vma=False,
    )
```
